512 devices in a mesh: group: 8 (over z_hi, y), dp: 8 (over z_lo), tensor: 8 (over x, core).
Axes of the slice: x: 4, y: 4, z: 16 (z_hi: 2, z_lo: 8; z = z_hi * 8 + z_lo), core: 2. Of those that a mesh axis runs over, the one named last changes fastest.
Arguments:
- hidden: bfloat16 [4, 4096, 5120], P(None, ('group', 'dp'), 'tensor'), may hold values from -6 to 6
- cache: bfloat16 [4096, 8, 128, 256], P(('group', 'dp'), 'tensor'), as said below
- lengths: int32 [4096], P(('group', 'dp')), may hold values from 1 to 128, as said below
- norm_gain: float32 [5120], replicated, may hold values from 0.1 to 1.9
- w_qkv: bfloat16 [5120, 5120], P(('group', 'dp'), 'tensor'), may hold values from -0.078125 to 0.078125
- qkv_bias: float32 [5120], P('tensor'), may hold values from -3 to 3
- w_out: bfloat16 [5120, 3072], P(('group', 'dp'), 'tensor'), may hold values from -0.109375 to 0.109375
Outputs:
- attended: bfloat16 [4, 4096, 5120], P(None, ('group', 'dp'), 'tensor')
The draws below stay inside these ranges and needn't reach their ends.
Inputs may be any that keep to these rules, and one draw needn't show every extreme that they name: `cache`: the first 128 entries of the last dimension are keys, the rest values; positions at or beyond a sequence's length are never read. `lengths`: the first of each device's 64 sequences holds all 128 positions.
All inputs are finite; a program needn't handle non-finite values.
Results may differ from the reference program's by a relative error of at most 0.018.
Values may be sent and summed in bfloat16 or wider, within the bound.
A program may use at most 64 MiB of HBM per device.

```python
import jax
import jax.numpy as jnp
from jax import lax

D = 5120
KVH = 8
HD = 128
QPK = 3
STEPS = 4
ROWS_DEV = 64
CACHE = 128
ROWS = 4096
QKV = 5120
OUTW = 3072
N_TENSOR = 8


def draw_cache(key, part):
    key = jax.random.fold_in(key, 11)
    first_key = jax.random.fold_in(key, 0)
    base = jax.random.normal(first_key, (ROWS, KVH, CACHE, 2 * HD), jnp.float32)
    result = base
    return result.astype(jnp.bfloat16)


def draw_lengths(key, part):
    key = jax.random.fold_in(key, 23)
    drawn = jax.random.randint(key, (ROWS,), 1, CACHE + 1, jnp.int32)
    leading = jnp.arange(ROWS, dtype=jnp.int32) % ROWS_DEV == 0
    return jnp.where(leading, CACHE, drawn).astype(jnp.int32)


def levels(rng, dims, shards, low, top_value):
    def one(axis_at, parts):
        draws = jax.random.uniform(jax.random.fold_in(jax.random.fold_in(rng, 6), axis_at), (parts,), jnp.float32, low / len(shards), top_value / len(shards))
        return jnp.repeat(jnp.exp(draws), dims[axis_at] // parts).reshape((-1,) + (1,) * (len(dims) - axis_at - 1))

    loudness = one(*shards[0])
    for cut in shards[1:]:
        loudness = loudness * one(*cut)
    return loudness


def normal_values(key, extent, deviation, most, shards=(), kind=jnp.bfloat16):
    factor_of = levels(key, extent, shards, -0.22, 0.18) if shards else 1.0
    values = jax.random.normal(key, extent, jnp.float32) * deviation * factor_of
    return jnp.minimum(jnp.maximum(values, -most), most).astype(kind)


def setup_inputs(seed: int = 0) -> dict:
    splits = jax.random.split(jax.random.key(seed), 8)
    return {
        "hidden": normal_values(splits[0], (STEPS, ROWS, D), 1.0, 6.0, ((1, 64), (2, 8))),
        "cache": draw_cache(jax.random.fold_in(splits[7], 71), 0),
        "lengths": draw_lengths(jax.random.fold_in(splits[7], 71), 0),
        "norm_gain": jnp.clip(1.0 + 0.18 * jax.random.normal(splits[3], (D,), jnp.float32), 0.1, 1.9),
        "w_qkv": normal_values(splits[4], (D, QKV), D ** -0.5, 0.078125, ((0, 64), (1, 8))),
        "qkv_bias": normal_values(splits[5], (QKV,), 0.5, 3.0, ((0, 8),), jnp.float32),
        "w_out": normal_values(splits[6], (D, OUTW), OUTW ** -0.5, 0.109375, ((0, 64), (1, 8))),
    }


ROPE_BASE = 1000000.0
NEG_FILL = -1e+30
NORM_EPS = 1e-06

def rotate(vectors, places):
    half = vectors.shape[-1] // 2
    inverse = ROPE_BASE ** (-(jnp.arange(half, dtype=jnp.float32) * 2.0 / vectors.shape[-1]))
    angles = places[..., None] * inverse
    cosine = jnp.cos(angles)
    sine_part = jnp.sin(angles)
    first_half = vectors[..., :half]
    second_half = vectors[..., half:]
    return jnp.concatenate([first_half * cosine - second_half * sine_part, second_half * cosine + first_half * sine_part], axis=-1)

def attend(queries, new_keys, new_values, cached, lengths):
    head_size = queries.shape[-1]
    num_steps = queries.shape[0]
    span = cached.shape[2]
    score_scale = head_size ** (-0.5)
    cache_keys = cached[..., :head_size].astype(jnp.float32)
    cache_values = cached[..., head_size:].astype(jnp.float32)
    query_f = queries.astype(jnp.float32)
    old_scores = jnp.einsum('srhqd,rhcd->srhqc', query_f, cache_keys) * score_scale
    live = jnp.arange(span, dtype=jnp.int32)[None, :] < lengths[:, None]
    old_scores = jnp.where(live[None, :, None, None, :], old_scores, NEG_FILL)
    fresh_scores = jnp.einsum('srhqd,urhd->srhqu', query_f, new_keys.astype(jnp.float32)) * score_scale
    causal = jnp.arange(num_steps, dtype=jnp.int32)[None, :] <= jnp.arange(num_steps, dtype=jnp.int32)[:, None]
    fresh_scores = jnp.where(causal[:, None, None, None, :], fresh_scores, NEG_FILL)
    scores = jnp.concatenate([old_scores, fresh_scores], axis=-1)
    highest = lax.optimization_barrier(jnp.max(scores, axis=-1, keepdims=True))
    weights = jnp.exp(scores - highest)
    weights = (weights / lax.optimization_barrier(jnp.sum(weights, axis=-1, keepdims=True))).astype(jnp.bfloat16)
    mixed = jnp.einsum('srhqc,rhcd->srhqd', weights[..., :span].astype(jnp.float32), cache_values)
    mixed = mixed + jnp.einsum('srhqu,urhd->srhqd', weights[..., span:].astype(jnp.float32), new_values.astype(jnp.float32))
    return mixed.astype(jnp.bfloat16)

def reference(hidden, cache, lengths, norm_gain, w_qkv, qkv_bias, w_out):
    source = hidden.astype(jnp.float32)
    mean_square = lax.optimization_barrier(jnp.mean(source * source, axis=-1, keepdims=True))
    normed = (source * lax.rsqrt(mean_square + NORM_EPS) * norm_gain).astype(jnp.bfloat16)
    projected = jnp.dot(normed.reshape(STEPS * ROWS, D), w_qkv, preferred_element_type=jnp.float32) + qkv_bias
    projected = projected.reshape(STEPS, ROWS, KVH, QPK + 2, HD)
    places = (lengths[None, :] + jnp.arange(STEPS, dtype=jnp.int32)[:, None]).astype(jnp.float32)
    queries = rotate(projected[:, :, :, :QPK, :], places[:, :, None, None]).astype(jnp.bfloat16)
    new_keys = rotate(projected[:, :, :, QPK, :], places[:, :, None]).astype(jnp.bfloat16)
    new_values = projected[:, :, :, QPK + 1, :].astype(jnp.bfloat16)
    per_rank = KVH // N_TENSOR
    columns = per_rank * QPK * HD

    def add_rank(total, rank):
        first_head = (rank * per_rank).astype(jnp.int32)
        mixed = attend(lax.dynamic_slice_in_dim(queries, first_head, per_rank, 2), lax.dynamic_slice_in_dim(new_keys, first_head, per_rank, 2), lax.dynamic_slice_in_dim(new_values, first_head, per_rank, 2), lax.dynamic_slice_in_dim(cache, first_head, per_rank, 1), lengths)
        flat = mixed.reshape(STEPS * ROWS, columns)
        block = lax.dynamic_slice_in_dim(w_out, (first_head * (QPK * HD)).astype(jnp.int32), columns, 1)
        term = lax.dot_general(flat, block, (((1,), (1,)), ((), ())), preferred_element_type=jnp.float32)
        term = lax.optimization_barrier(term.astype(jnp.bfloat16)).astype(jnp.float32)
        return (total + term, None)
    total, _ = lax.scan(add_rank, jnp.zeros((STEPS * ROWS, D), jnp.float32), jnp.arange(N_TENSOR, dtype=jnp.int32))
    return total.astype(jnp.bfloat16).reshape(STEPS, ROWS, D)
```

```python
import functools

import jax
import jax.numpy as jnp
import numpy as np
from jax import lax
from jax.experimental import pallas as pl
from jax.experimental.pallas import tpu as pltpu
from jax.sharding import PartitionSpec as P

MESH = pl.DeviceIdType.MESH
BF, F32 = jnp.bfloat16, jnp.float32
NT = (((1,), (1,)), ((), ()))
ROPE_BASE = 1000000.0
NEG = -1e30
EPS = 1e-6
NY, NZ, NX = 4, 16, 4
ROWS = 64
STEPS = 4
TOK = STEPS * ROWS
HD = 128
QPK = 3
DEEP = 80
FEAT = 640
OUTC = QPK * HD
ACUT = 48
OFFS = (0, 1, 3, 2)


def kernel(
    hidden_ref, cache_ref, lens_ref, gain_ref, wq_ref, bias_ref, wo_ref, freq_ref, out_ref,
    hid, cache, hg, xs, wq, wo, ssb, ps, pr, osb, orb, xsb, xrb, qs, sc, mx, rope_c, rope_s, rcol, acc,
    loc_sem, h1, hx, hs, hh, hsend, zs, zsend, ss_sem, rs, rss, oa, ob, oby, oy, osend, od, ods, xr, xss,
):
    g, d, t = lax.axis_index("group"), lax.axis_index("dp"), lax.axis_index("tensor")
    y, z = lax.rem(g, 4), (g // 4) * 8 + d
    x, c = t // 2, lax.rem(t, 2)

    def dev(dy=0, dz=0, dx=0, flip=False):
        yy, zz, xx = lax.rem(y + dy + NY, NY), lax.rem(z + dz + NZ, NZ), lax.rem(x + dx + NX, NX)
        return ((zz // 8) * 4 + yy, lax.rem(zz, 8), 2 * xx + ((1 - c) if flip else c))

    def slot(dy=0, dz=0):
        yy, zz = lax.rem(y + dy + NY, NY), lax.rem(z + dz + NZ, NZ)
        return ((zz // 8) * 4 + yy) * 8 + lax.rem(zz, 8)

    def send(src, dst, ssem, rsem, where):
        pltpu.make_async_remote_copy(
            src_ref=src, dst_ref=dst, send_sem=ssem, recv_sem=rsem, device_id=where, device_id_type=MESH
        ).start()

    def wait(ref, sem):
        pltpu.make_async_copy(ref, ref, sem).wait()

    loads = [
        pltpu.make_async_copy(hidden_ref, hid, loc_sem.at[0]),
        pltpu.make_async_copy(wq_ref, wq.at[z], loc_sem.at[1]),
        pltpu.make_async_copy(wo_ref, wo.at[slot()], loc_sem.at[2]),
        pltpu.make_async_copy(cache_ref, cache, loc_sem.at[3]),
    ]
    for copy in loads:
        copy.start()
    barrier = pltpu.get_barrier_semaphore()
    friends = [dev(dy=1), dev(dy=2), dev(dy=3), dev(dz=1), dev(dz=-1), dev(flip=True)]
    for dx in (1, 2, 3):
        friends += [dev(dx=dx), dev(dx=dx, flip=True)]
    for friend in friends:
        pl.semaphore_signal(barrier, inc=1, device_id=friend, device_id_type=MESH)

    hub = (c == lax.rem(y, 2)) & (lax.rem(x, 2) == y // 2)
    relay = (c == lax.rem(y, 2)) & (lax.rem(x, 2) != y // 2)
    leaf = c != lax.rem(y, 2)
    kb = x // 2

    loads[0].wait()
    ones = jnp.ones((8, FEAT), F32)
    for s in range(STEPS):
        raw = hid[s].astype(F32)
        hg[s * ROWS : (s + 1) * ROWS, :] = (raw * gain_ref[...]).astype(BF)
        ssb[t, :, s * ROWS : (s + 1) * ROWS] = lax.dot_general(
            ones, raw * raw, NT, preferred_element_type=F32, precision=lax.Precision.HIGHEST
        )

    @pl.when(hub)
    def _():
        xs[kb, y] = hg[...]

    loads[1].wait()
    pl.semaphore_wait(barrier, len(friends))

    cuts = ((0, ACUT), (ACUT, DEEP - ACUT))

    def z_send(way, zz, piece, k):
        lo, n = cuts[piece]
        ref = wq.at[zz, pl.ds(lo, n)]
        send(ref, ref, zsend, zs.at[way, k - 1, piece], dev(dz=1 if way == 0 else -1))

    def z_step(k):
        for piece in (0, 1):
            for way in (0, 1):
                if k == 8 and piece != way:
                    continue
                zz = lax.rem(z + (NZ - k if way == 0 else k), NZ)
                lo, n = cuts[piece]
                wait(wq.at[zz, pl.ds(lo, n)], zs.at[way, k - 1, piece])
                if k < 7 or (k == 7 and piece == way):
                    z_send(way, zz, piece, k + 1)

    def h_order(j):
        return lax.rem(y + OFFS[j], NY)

    def hub_event(j):
        @pl.when(hub)
        def _():
            ys = h_order(j)
            block = xs.at[kb, ys]
            if j:
                wait(block, h1.at[ys])
            send(block, block, hsend.at[0], hx.at[kb, ys], dev(dx=1))
            send(block, block, hsend.at[0], hx.at[kb, ys], dev(dx=-1))
            send(block, block, hsend.at[1], hs.at[kb, ys], dev(flip=True))

    def relay_event(j):
        @pl.when(relay)
        def _():
            ys = h_order(j)
            for side in (-1, 1):
                kbs = lax.rem(x + side + NX, NX) // 2
                block = xs.at[kbs, ys]
                wait(block, hx.at[kbs, ys])
                half = 0 if side == -1 else 1
                part = xs.at[kbs, ys, pl.ds(half * (TOK // 2), TOK // 2)]
                send(part, part, hsend.at[0], hh.at[half, ys], dev(dx=-side))
                send(block, block, hsend.at[1], hs.at[kbs, ys], dev(flip=True))

    def far_event(j):
        @pl.when(hub)
        def _():
            ys = h_order(j)
            for half in (0, 1):
                wait(xs.at[1 - kb, ys, pl.ds(half * (TOK // 2), TOK // 2)], hh.at[half, ys])
            block = xs.at[1 - kb, ys]
            send(block, block, hsend.at[1], hs.at[1 - kb, ys], dev(flip=True))

    def o_y(ref):
        for dy in (2, 1, 3):
            send(ref, ref, osend, oy, dev(dy=dy))

    def o_zsend(way, ref, sem):
        send(ref, ref, osend, sem, dev(dz=1 if way == 0 else -1))

    def o_start():
        part = wo.at[slot(), pl.ds(ACUT, DEEP - ACUT)]
        for j in (3, 1, 2):
            send(part, part, osend, oby.at[j], dev(dy=OFFS[j]))
        for way in (0, 1):
            o_zsend(way, part, ob.at[way, 0, 0])
        part = wo.at[slot(), pl.ds(0, ACUT)]
        for way in (0, 1):
            o_zsend(way, part, oa.at[way, 0])
        o_y(part)

    def o_rows():
        for j in (1, 2, 3):
            part = wo.at[slot(dy=-OFFS[j]), pl.ds(ACUT, DEEP - ACUT)]
            wait(part, oby.at[j])
            for way in (0, 1):
                o_zsend(way, part, ob.at[way, j, 0])

    acuts = ((0, 32), (32, 16))
    bcuts = ((ACUT, 16), (ACUT + 16, 16))

    def o_step(k):
        for way in (0, 1):
            home = slot(dz=-k if way == 0 else k)
            lo, n = acuts[way] if k == 8 else (0, ACUT)
            wait(wo.at[home, pl.ds(lo, n)], oa.at[way, k - 1])
            if k < 8:
                lo, n = acuts[way] if k == 7 else (0, ACUT)
                o_zsend(way, wo.at[home, pl.ds(lo, n)], oa.at[way, k])
        for j in range(4):
            for way in (0, 1):
                home = slot(dy=-OFFS[j], dz=-k if way == 0 else k)
                lo, n = bcuts[way] if k == 8 else (ACUT, DEEP - ACUT)
                wait(wo.at[home, pl.ds(lo, n)], ob.at[way, j, k - 1])
                if k < 8:
                    lo, n = bcuts[way] if k == 7 else (ACUT, DEEP - ACUT)
                    o_zsend(way, wo.at[home, pl.ds(lo, n)], ob.at[way, j, k])
        for way in (0, 1):
            if k < 8 or way == 0:
                o_y(wo.at[slot(dz=-k if way == 0 else k), pl.ds(0, ACUT)])

    for piece in (0, 1):
        for way in (0, 1):
            z_send(way, z, piece, 1)

    @pl.when(jnp.logical_not(hub))
    def _():
        yt = lax.rem(t, NY)
        send(hg, xs.at[kb, y], hsend.at[2], h1.at[y], dev(dy=yt - y))

    hub_event(0)
    for friend in friends[5:]:
        send(ssb.at[t], ssb.at[t], ss_sem.at[0], ss_sem.at[1], friend)
    loads[2].wait()

    eye = (
        lax.broadcasted_iota(jnp.int32, (ROWS, ROWS), 0) == lax.broadcasted_iota(jnp.int32, (ROWS, ROWS), 1)
    ).astype(BF)
    lens_b = lax.dot_general(
        eye,
        jnp.broadcast_to(lens_ref[...].astype(F32), (HD, ROWS)).astype(BF),
        NT,
        preferred_element_type=F32,
    )
    lane = lax.broadcasted_iota(jnp.int32, (ROWS, HD), 1)
    for s in range(STEPS):
        angle = (lens_b + float(s)) * freq_ref[...]
        rope_c[s * ROWS : (s + 1) * ROWS, :] = jnp.cos(angle)
        sine = jnp.sin(angle)
        rope_s[s * ROWS : (s + 1) * ROWS, :] = jnp.where(lane < HD // 2, -sine, sine)

    for k in range(1, 9):
        z_step(k)
        if k == 2:
            hub_event(1)
            relay_event(0)
        if k == 3:
            hub_event(2)
            hub_event(3)
            relay_event(1)
            o_start()
        if k == 4:
            far_event(0)
            o_rows()
        if k == 5:
            relay_event(2)
            far_event(1)
            o_step(1)
        if k == 6:
            relay_event(3)
            far_event(2)
        if k == 7:
            far_event(3)
            o_step(2)

    @pl.when(leaf)
    def _():
        for j in range(4):
            for kk in (0, 1):
                wait(xs.at[kk, h_order(j)], hs.at[kk, h_order(j)])

    def product(ys):
        total = jnp.zeros((TOK, FEAT), F32)
        for kk in (0, 1):
            total += jnp.dot(
                xs[kk, ys], wq[kk * 8 : (kk + 1) * 8].reshape(8 * DEEP, FEAT), preferred_element_type=F32
            )
        return total

    for j, dy in enumerate((2, 1, 3)):
        ps[j] = product(lax.rem(y + dy, NY)).astype(BF)
        send(ps.at[j], pr.at[j], rss.at[j], rs.at[j], dev(dy=dy))
    acc[...] = product(y)

    wait(ssb.at[0:7], ss_sem.at[1])
    whole = jnp.sum(ssb[...], axis=0)[0:1, :] * (1.0 / (8 * FEAT))
    scale = lax.rsqrt(whole + EPS)
    eye_t = (
        lax.broadcasted_iota(jnp.int32, (TOK, TOK), 0) == lax.broadcasted_iota(jnp.int32, (TOK, TOK), 1)
    ).astype(F32)
    rcol[...] = lax.dot_general(
        eye_t,
        jnp.broadcast_to(scale, (HD, TOK)),
        NT,
        preferred_element_type=F32,
        precision=lax.Precision.HIGHEST,
    )
    o_step(3)
    o_step(4)
    for j in (1, 2, 0):
        wait(pr.at[j], rs.at[j])
        acc[...] += pr[j].astype(F32)

    def head(i):
        cols = slice(i * HD, (i + 1) * HD)
        return acc[:, cols] * rcol[...] + bias_ref[:, cols]

    def rotate(v):
        return v * rope_c[...] + pltpu.roll(v, HD // 2, 1) * rope_s[...]

    for i in range(QPK):
        qs[i * TOK : (i + 1) * TOK, :] = rotate(head(i)).astype(BF).astype(F32)
    new_k = rotate(head(QPK)).astype(BF)
    new_v = head(QPK + 1).astype(BF)
    o_step(5)

    loads[3].wait()
    nq = STEPS * QPK

    def old_scores(r, _):
        q = qs[pl.ds(r, nq, stride=ROWS), :].astype(BF)
        sc[pl.ds(r, nq, stride=ROWS), :] = lax.dot_general(
            q, cache[r, :, 0:HD], NT, preferred_element_type=F32
        )
        return _

    lax.fori_loop(0, ROWS, old_scores, 0, unroll=8)
    factor = HD ** (-0.5)
    live = lax.broadcasted_iota(jnp.int32, (ROWS, HD), 1).astype(F32) < lens_b
    row = lax.broadcasted_iota(jnp.int32, (ROWS, TOK), 0)
    col = lax.broadcasted_iota(jnp.int32, (ROWS, TOK), 1)
    mine = lax.rem(col, ROWS) == row
    for i in range(nq):
        s = i % STEPS
        rows = slice(i * ROWS, (i + 1) * ROWS)
        old = jnp.where(live, sc[rows, :] * factor, NEG)
        fresh = (
            lax.dot_general(qs[rows, :].astype(BF), new_k, NT, preferred_element_type=F32) * factor
        )
        fresh = jnp.where(mine & (col < (s + 1) * ROWS), fresh, NEG)
        top = jnp.maximum(jnp.max(old, axis=1, keepdims=True), jnp.max(fresh, axis=1, keepdims=True))
        old = jnp.exp(old - top)
        fresh = jnp.exp(fresh - top)
        total = jnp.sum(old, axis=1, keepdims=True) + jnp.sum(fresh, axis=1, keepdims=True)
        sc[rows, :] = (old / total).astype(BF).astype(F32)
        mx[rows, :] = jnp.dot((fresh / total).astype(BF), new_v, preferred_element_type=F32)

    def old_values(r, _):
        p = sc[pl.ds(r, nq, stride=ROWS), :].astype(BF)
        mx[pl.ds(r, nq, stride=ROWS), :] += jnp.dot(p, cache[r, :, HD:], preferred_element_type=F32)
        return _

    o_step(6)
    lax.fori_loop(0, ROWS, old_values, 0, unroll=8)
    mixed = jnp.concatenate([mx[i * TOK : (i + 1) * TOK, :].astype(BF) for i in range(QPK)], axis=1)
    o_step(7)
    o_step(8)
    wait(wo.at[0:48, pl.ds(0, ACUT)], oy)

    def partial_out(index):
        block = wo[pl.ds(index * 8, 8)].reshape(8 * DEEP, OUTC)
        return lax.dot_general(mixed, block, NT, preferred_element_type=F32)

    for j, dx in enumerate((2, 1, 3, 0)):
        osb[j] = partial_out(2 * lax.rem(x + dx, NX) + 1 - c).astype(BF)
        send(osb.at[j], orb.at[j], ods.at[j], od.at[j], dev(flip=True))
    for j, dx in enumerate((2, 1, 3, 0)):
        total = partial_out(2 * lax.rem(x + dx, NX) + c)
        wait(orb.at[j], od.at[j])
        total += orb[j].astype(F32)
        if j < 3:
            xsb[j] = total.astype(BF)
            send(xsb.at[j], xrb.at[j], xss.at[j], xr.at[j], dev(dx=dx))
        else:
            acc[...] = total
    for j in (1, 2, 0):
        wait(xrb.at[j], xr.at[j])
        acc[...] += xrb[j].astype(F32)
    out_ref[...] = acc[...].astype(BF).reshape(STEPS, ROWS, FEAT)

    wait(wq.at[0:15], zsend)
    wait(wo.at[0:63], osend)
    wait(ssb.at[0:7], ss_sem.at[0])

    @pl.when(hub)
    def _():
        wait(xs, hsend.at[0])

    @pl.when(relay)
    def _():
        wait(xs.at[0], hsend.at[0])

    @pl.when(jnp.logical_not(leaf))
    def _():
        wait(xs, hsend.at[1])

    @pl.when(jnp.logical_not(hub))
    def _():
        wait(hg, hsend.at[2])

    for j in range(3):
        wait(ps.at[j], rss.at[j])
        wait(xsb.at[j], xss.at[j])
    for j in range(4):
        wait(osb.at[j], ods.at[j])


def on_device(hidden, cache, lengths, norm_gain, w_qkv, qkv_bias, w_out):
    t = lax.axis_index("tensor")
    gain = lax.dynamic_slice_in_dim(norm_gain, t * FEAT, FEAT).reshape(1, FEAT)
    half = np.arange(HD // 2, dtype=np.float32) * np.float32(2.0 / HD)
    freq = np.power(np.float32(ROPE_BASE), -half).astype(np.float32)
    freq = jnp.asarray(np.concatenate([freq, freq])[None, :])
    dma = pltpu.SemaphoreType.DMA
    vmem, hbm = pl.BlockSpec(memory_space=pltpu.VMEM), pl.BlockSpec(memory_space=pl.ANY)
    nq = STEPS * QPK * ROWS
    return pl.pallas_call(
        kernel,
        out_shape=jax.ShapeDtypeStruct((STEPS, ROWS, FEAT), BF),
        in_specs=[hbm, hbm, vmem, vmem, hbm, vmem, hbm, vmem],
        out_specs=vmem,
        scratch_shapes=[
            pltpu.VMEM((STEPS, ROWS, FEAT), BF),
            pltpu.VMEM((ROWS, 128, 2 * HD), BF),
            pltpu.VMEM((TOK, FEAT), BF),
            pltpu.VMEM((2, NY, TOK, FEAT), BF),
            pltpu.VMEM((NZ, DEEP, FEAT), BF),
            pltpu.VMEM((NY * NZ, DEEP, OUTC), BF),
            pltpu.VMEM((8, 8, TOK), F32),
            pltpu.VMEM((3, TOK, FEAT), BF),
            pltpu.VMEM((3, TOK, FEAT), BF),
            pltpu.VMEM((4, TOK, FEAT), BF),
            pltpu.VMEM((4, TOK, FEAT), BF),
            pltpu.VMEM((3, TOK, FEAT), BF),
            pltpu.VMEM((3, TOK, FEAT), BF),
            pltpu.VMEM((nq, HD), F32),
            pltpu.VMEM((nq, HD), F32),
            pltpu.VMEM((nq, HD), F32),
            pltpu.VMEM((TOK, HD), F32),
            pltpu.VMEM((TOK, HD), F32),
            pltpu.VMEM((TOK, HD), F32),
            pltpu.VMEM((TOK, FEAT), F32),
            dma((4,)),
            dma((NY,)),
            dma((2, NY)),
            dma((2, NY)),
            dma((2, NY)),
            dma((3,)),
            dma((2, 8, 2)),
            dma,
            dma((2,)),
            dma((3,)),
            dma((3,)),
            dma((2, 8)),
            dma((2, 4, 8)),
            dma((4,)),
            dma,
            dma,
            dma((4,)),
            dma((4,)),
            dma((3,)),
            dma((3,)),
        ],
        compiler_params=pltpu.CompilerParams(
            collective_id=0, has_side_effects=True, vmem_limit_bytes=56 * 2**20
        ),
    )(
        hidden,
        cache.reshape(ROWS, 128, 2 * HD),
        lengths.reshape(1, ROWS),
        gain,
        w_qkv,
        qkv_bias.reshape(1, FEAT),
        w_out,
        freq,
    )


def solution(mesh):
    placed = (
        P(None, ("group", "dp"), "tensor"),
        P(("group", "dp"), "tensor", None, None),
        P(("group", "dp")),
        P(),
        P(("group", "dp"), "tensor"),
        P("tensor"),
        P(("group", "dp"), "tensor"),
    )
    return jax.shard_map(
        on_device,
        mesh=mesh,
        in_specs=placed,
        out_specs=P(None, ("group", "dp"), "tensor"),
        check_vma=False,
    )
```

```python
import functools

import jax
import jax.numpy as jnp
import numpy as np
from jax import lax
from jax.experimental import pallas as pl
from jax.experimental.pallas import tpu as pltpu
from jax.sharding import PartitionSpec as P

MESH = pl.DeviceIdType.MESH
BF, F32 = jnp.bfloat16, jnp.float32
NT = (((1,), (1,)), ((), ()))
ROPE_BASE = 1000000.0
NEG = -1e30
EPS = 1e-6
NY, NZ, NX = 4, 16, 4
ROWS = 64
STEPS = 4
TOK = STEPS * ROWS
HD = 128
HALF = 32
HTOK = STEPS * HALF
QPK = 3
DEEP = 80
FEAT = 640
OUTC = QPK * HD
ACUT = 64
ZCUTS = ((0, 32), (32, 32), (64, 16))
OFFS = (0, 1, 3, 2)
PLAN = {
    1: [("oa", 1), ("oy", 1), ("of", 0), ("hub", 1, 0), ("hub", 2, 0), ("relay", 0, 0)],
    2: [("oa", 2), ("oy", 2), ("of", 1), ("hub", 1, 1), ("hub", 2, 1), ("hub", 3, 0), ("relay", 0, 1), ("ob", 0)],
    3: [("oa", 3), ("oy", 3), ("of", 2), ("hub", 3, 1), ("relay", 1, 0), ("relay", 2, 0), ("far", 0, 0), ("far", 0, 1), ("rope", 0, 0), ("rope", 0, 1)],
    4: [("oa", 4), ("oy", 4), ("of", 3), ("relay", 1, 1), ("relay", 2, 1), ("far", 1, 0), ("far", 2, 0), ("rope", 0, 2), ("rope", 0, 3), ("ob", 1)],
    5: [("oa", 5), ("oy", 5), ("of", 4), ("relay", 3, 0), ("relay", 3, 1), ("rope", 1, 0), ("rope", 1, 1), ("ob", 2)],
    6: [("oa", 6), ("oy", 6), ("of", 5), ("far", 1, 1), ("far", 2, 1), ("far", 3, 0), ("far", 3, 1), ("rope", 1, 2), ("rope", 1, 3), ("ob", 3)],
    7: [("oa", 7), ("oy", 7), ("of", 6), ("ob", 4)],
    8: [("oa", 8), ("oy", 8), ("of", 7), ("ob", 5)],
    "sent": [("of", 8), ("ob", 6)],
    "back": [("ob", 7)],
    "first": [("ob", 8)],
}


def kernel(
    hidden_ref, cache_ref, lens_ref, gain_ref, wq_ref, bias_ref, wo_ref, freq_ref, out_ref,
    gain, bias, lens, freq, hid, cache, hg, xs, wq, wo, ssb, ps, pr, osb, orb, xsb, xrb, qs, sc, mx, rope_c, rope_s, rcol, acc,
    loc_sem, h1, hx, hs, hh, hsend, zs, zsend, ss_sem, rs, rss, oa, ob, oby, oyf, oy, osend, od, ods, xr, xss,
):
    g, d, t = lax.axis_index("group"), lax.axis_index("dp"), lax.axis_index("tensor")
    y, z = lax.rem(g, 4), (g // 4) * 8 + d
    x, c = t // 2, lax.rem(t, 2)

    def dev(dy=0, dz=0, dx=0, flip=False):
        yy, zz, xx = lax.rem(y + dy + NY, NY), lax.rem(z + dz + NZ, NZ), lax.rem(x + dx + NX, NX)
        return ((zz // 8) * 4 + yy, lax.rem(zz, 8), 2 * xx + ((1 - c) if flip else c))

    def slot(dy=0, dz=0):
        yy, zz = lax.rem(y + dy + NY, NY), lax.rem(z + dz + NZ, NZ)
        return ((zz // 8) * 4 + yy) * 8 + lax.rem(zz, 8)

    def send(src, dst, ssem, rsem, where):
        pltpu.make_async_remote_copy(
            src_ref=src, dst_ref=dst, send_sem=ssem, recv_sem=rsem, device_id=where, device_id_type=MESH
        ).start()

    def wait(ref, sem):
        pltpu.make_async_copy(ref, ref, sem).wait()

    loads = [
        pltpu.make_async_copy(hidden_ref, hid, loc_sem.at[0]),
        pltpu.make_async_copy(wq_ref, wq.at[z], loc_sem.at[1]),
        pltpu.make_async_copy(wo_ref, wo.at[slot()], loc_sem.at[2]),
        pltpu.make_async_copy(cache_ref, cache, loc_sem.at[3]),
        pltpu.make_async_copy(gain_ref, gain, loc_sem.at[4]),
        pltpu.make_async_copy(bias_ref, bias, loc_sem.at[5]),
        pltpu.make_async_copy(lens_ref, lens, loc_sem.at[6]),
        pltpu.make_async_copy(freq_ref, freq, loc_sem.at[7]),
    ]
    for copy in loads[1:2] + loads[:1] + loads[4:] + loads[2:4]:
        copy.start()
    barrier = pltpu.get_barrier_semaphore()
    friends = [dev(dy=1), dev(dy=2), dev(dy=3), dev(dz=1), dev(dz=-1), dev(flip=True)]
    for dx in (1, 2, 3):
        friends += [dev(dx=dx), dev(dx=dx, flip=True)]
    for friend in friends:
        pl.semaphore_signal(barrier, inc=1, device_id=friend, device_id_type=MESH)

    hub = (c == lax.rem(y, 2)) & (lax.rem(x, 2) == y // 2)
    relay = (c == lax.rem(y, 2)) & (lax.rem(x, 2) != y // 2)
    leaf = c != lax.rem(y, 2)
    kb = x // 2

    loads[1].wait()
    pl.semaphore_wait(barrier, len(friends))

    pieces = len(ZCUTS)

    def z_part(zz, piece):
        lo, n = ZCUTS[piece]
        return wq.at[zz, pl.ds(lo, n)]

    def z_send(way, zz, piece, k):
        send(z_part(zz, piece), z_part(zz, piece), zsend, zs.at[way, k - 1, piece], dev(dz=1 if way == 0 else -1))

    def z_last(way, piece):
        return (piece < pieces // 2) == (way == 1)

    def z_step(k):
        for piece in range(pieces):
            for way in (0, 1):
                if k == 8 and not z_last(way, piece):
                    continue
                zz = lax.rem(z + (NZ - k if way == 0 else k), NZ)
                wait(z_part(zz, piece), zs.at[way, k - 1, piece])
                if k < 7 or (k == 7 and z_last(way, piece)):
                    z_send(way, zz, piece, k + 1)

    def h_part(kbs, j, h, lo=0, n=HTOK):
        return xs.at[kbs, lax.rem(y + OFFS[j], NY), pl.ds(h * HTOK + lo, n)]

    def hub_event(j, h):
        @pl.when(hub)
        def _():
            part = h_part(kb, j, h)
            if j:
                wait(part, h1.at[j, h])
            send(part, part, hsend.at[0], hx.at[kb, j, h], dev(dx=1))
            send(part, part, hsend.at[0], hx.at[kb, j, h], dev(dx=-1))
            send(part, part, hsend.at[1], hs.at[kb, j, h], dev(flip=True))

    def relay_event(j, h):
        @pl.when(relay)
        def _():
            for side in (-1, 1):
                kbs = lax.rem(x + side + NX, NX) // 2
                part = h_part(kbs, j, h)
                wait(part, hx.at[kbs, j, h])
                far = 0 if side == -1 else 1
                piece = h_part(kbs, j, h, far * (HTOK // 2), HTOK // 2)
                send(piece, piece, hsend.at[0], hh.at[far, j, h], dev(dx=-side))
                send(part, part, hsend.at[1], hs.at[kbs, j, h], dev(flip=True))

    def far_event(j, h):
        @pl.when(hub)
        def _():
            for far in (0, 1):
                wait(h_part(1 - kb, j, h, far * (HTOK // 2), HTOK // 2), hh.at[far, j, h])
            part = h_part(1 - kb, j, h)
            send(part, part, hsend.at[1], hs.at[1 - kb, j, h], dev(flip=True))

    def o_y(k, way):
        part = wo.at[slot(dz=-k if way == 0 else k), pl.ds(0, ACUT)]
        send(part, part, osend, oyf.at[0, k] if way == 0 and k < 8 else oy, dev(dy=1))
        send(part, part, osend, oyf.at[1, k] if (way == 1 and k > 0) or k == 8 else oy, dev(dy=-1))

    def o_yfwd(k):
        for way in (0, 1):
            if k == 0 and way == 1 or k == 8 and way == 0:
                continue
            part = wo.at[slot(dy=-1 if way == 0 else 1, dz=-k if way == 0 else k), pl.ds(0, ACUT)]
            wait(part, oyf.at[way, k])
            send(part, part, osend, oy, dev(dy=1 if way == 0 else -1))

    def o_zsend(way, ref, sem):
        send(ref, ref, osend, sem, dev(dz=1 if way == 0 else -1))

    def o_start():
        part = wo.at[slot(), pl.ds(ACUT, DEEP - ACUT)]
        for j in (3, 1, 2):
            send(part, part, osend, oby.at[j], dev(dy=OFFS[j]))
        part = wo.at[slot(), pl.ds(0, ACUT)]
        for way in (0, 1):
            o_zsend(way, part, oa.at[way, 0])
        o_y(0, 0)

    def ob_start():
        for j in (0, 1, 2, 3):
            part = wo.at[slot(dy=-OFFS[j]), pl.ds(ACUT, DEEP - ACUT)]
            if j:
                wait(part, oby.at[j])
            for way in (0, 1):
                o_zsend(way, part, ob.at[way, j, 0])

    acuts = ((0, 32), (32, 32))

    def oa_step(k):
        for way in (0, 1):
            home = slot(dz=-k if way == 0 else k)
            lo, n = acuts[way] if k == 8 else (0, ACUT)
            wait(wo.at[home, pl.ds(lo, n)], oa.at[way, k - 1])
            if k < 8:
                lo, n = acuts[way] if k == 7 else (0, ACUT)
                o_zsend(way, wo.at[home, pl.ds(lo, n)], oa.at[way, k])

    def oa_y(k):
        for way in (0, 1):
            if k < 8 or way == 0:
                o_y(k, way)

    def ob_step(k):
        for j in range(4):
            for way in (0, 1):
                if k == 8 and j % 2 != way:
                    continue
                part = wo.at[slot(dy=-OFFS[j], dz=-k if way == 0 else k), pl.ds(ACUT, DEEP - ACUT)]
                wait(part, ob.at[way, j, k - 1])
                if k < 7 or (k == 7 and j % 2 == way):
                    o_zsend(way, part, ob.at[way, j, k])

    for piece in range(pieces):
        for way in (0, 1):
            z_send(way, z, piece, 1)
    loads[0].wait()
    loads[4].wait()
    for i in range(FEAT // HD):
        cols = slice(i * HD, (i + 1) * HD)
        row = gain[pl.ds(t * (FEAT // HD) + i, 1), :]
        for h in (0, 1):
            part = hid[:, h * HALF : (h + 1) * HALF, cols].reshape(HTOK, HD)
            hg[h * HTOK : (h + 1) * HTOK, cols] = (part.astype(F32) * row).astype(BF)

    @pl.when(hub)
    def _():
        xs[kb, y] = hg[...]

    back_y = lax.rem(y - lax.rem(t, NY) + NY, NY)
    order = lax.rem(back_y * (5 * back_y - 3) // 2, NY)

    @pl.when(jnp.logical_not(hub))
    def _():
        for h in (0, 1):
            rows = pl.ds(h * HTOK, HTOK)
            send(hg.at[rows], xs.at[kb, y, rows], hsend.at[2], h1.at[order, h], dev(dy=-back_y))

    hub_event(0, 0)
    hub_event(0, 1)
    loads[2].wait()
    o_start()
    ones = jnp.ones((8, FEAT), F32)
    for h in (0, 1):
        raw = hid[:, h * HALF : (h + 1) * HALF, :].reshape(HTOK, FEAT).astype(F32)
        ssb[t, :, h * HTOK : (h + 1) * HTOK] = lax.dot_general(
            ones, raw * raw, NT, preferred_element_type=F32, precision=lax.Precision.HIGHEST
        )
    for friend in friends[5:]:
        send(ssb.at[t], ssb.at[t], ss_sem.at[0], ss_sem.at[1], friend)

    eye = (
        lax.broadcasted_iota(jnp.int32, (ROWS, ROWS), 0) == lax.broadcasted_iota(jnp.int32, (ROWS, ROWS), 1)
    ).astype(BF)
    loads[6].wait()
    loads[7].wait()
    lens_b = lax.dot_general(
        eye,
        jnp.broadcast_to(lens[...].astype(F32), (HD, ROWS)).astype(BF),
        NT,
        preferred_element_type=F32,
    )
    lane = lax.broadcasted_iota(jnp.int32, (HALF, HD), 1)

    def rope_table(h, s):
        rows = slice((h * STEPS + s) * HALF, (h * STEPS + s + 1) * HALF)
        angle = (lens_b[h * HALF : (h + 1) * HALF, :] + float(s)) * freq[...]
        rope_c[rows, :] = jnp.cos(angle)
        sine = jnp.sin(angle)
        rope_s[rows, :] = jnp.where(lane < HD // 2, -sine, sine)

    events = {
        "hub": hub_event,
        "relay": relay_event,
        "far": far_event,
        "oa": oa_step,
        "oy": oa_y,
        "of": o_yfwd,
        "ob": lambda k: ob_step(k) if k else ob_start(),
        "rope": rope_table,
    }

    def run(key):
        for name, *what in PLAN[key]:
            events[name](*what)

    for k in range(1, 9):
        z_step(k)
        run(k)

    @pl.when(leaf)
    def _():
        for j in range(4):
            for kk in (0, 1):
                for h in (0, 1):
                    wait(h_part(kk, j, h), hs.at[kk, j, h])

    def product(ys):
        total = jnp.zeros((TOK, FEAT), F32)
        for kk in (0, 1):
            total += jnp.dot(
                xs[kk, ys], wq[kk * 8 : (kk + 1) * 8].reshape(8 * DEEP, FEAT), preferred_element_type=F32
            )
        return total

    def rows_of(h):
        return slice(h * HTOK, (h + 1) * HTOK)

    def r_send(j, dy, h):
        rows = pl.ds(h * HTOK, HTOK)
        send(ps.at[j, rows], pr.at[j, rows], rss.at[j, h], rs.at[j, h], dev(dy=dy))

    ways = ((0, 2), (1, 1), (2, 3))
    for j, dy in ways:
        ps[j] = product(lax.rem(y + dy, NY)).astype(BF)
        r_send(j, dy, 0)
    for j, dy in ways:
        r_send(j, dy, 1)
    acc[...] = product(y)
    run("sent")

    wait(ssb.at[0:7], ss_sem.at[1])
    whole = jnp.sum(ssb[...], axis=0)[0:1, :] * (1.0 / (8 * FEAT))
    scale = lax.rsqrt(whole + EPS)
    eye_t = (
        lax.broadcasted_iota(jnp.int32, (TOK, TOK), 0) == lax.broadcasted_iota(jnp.int32, (TOK, TOK), 1)
    ).astype(F32)
    rcol[...] = lax.dot_general(
        eye_t,
        jnp.broadcast_to(scale, (HD, TOK)),
        NT,
        preferred_element_type=F32,
        precision=lax.Precision.HIGHEST,
    )
    run("back")
    loads[5].wait()
    loads[3].wait()

    nq = STEPS * QPK
    factor = HD ** (-0.5)
    span = lax.broadcasted_iota(jnp.int32, (HALF, HD), 1).astype(F32)
    fresh_row = lax.broadcasted_iota(jnp.int32, (HALF, HTOK), 0)
    fresh_col = lax.broadcasted_iota(jnp.int32, (HALF, HTOK), 1)
    mine = lax.rem(fresh_col, HALF) == fresh_row

    def attention(h):
        rows = rows_of(h)
        for j in (1, 2, 0):
            wait(pr.at[j, pl.ds(h * HTOK, HTOK)], rs.at[j, h])

        def head(i):
            cols = slice(i * HD, (i + 1) * HD)
            total = acc[rows, cols]
            for j in range(3):
                total += pr[j, rows, cols].astype(F32)
            return total * rcol[rows, :] + bias[i : i + 1, :]

        def rotate(v):
            return v * rope_c[rows, :] + pltpu.roll(v, HD // 2, 1) * rope_s[rows, :]

        for i in range(QPK):
            qs[i * HTOK : (i + 1) * HTOK, :] = rotate(head(i)).astype(BF).astype(F32)
        new_k = rotate(head(QPK)).astype(BF)
        new_v = head(QPK + 1).astype(BF)

        def old_scores(r, carry):
            q = qs[pl.ds(r, nq, stride=HALF), :].astype(BF)
            sc[pl.ds(r, nq, stride=HALF), :] = lax.dot_general(
                q, cache[h * HALF + r, :, 0:HD], NT, preferred_element_type=F32
            )
            return carry

        lax.fori_loop(0, HALF, old_scores, 0, unroll=32)
        live = span < lens_b[h * HALF : (h + 1) * HALF, :]
        for i in range(nq):
            s = i % STEPS
            part = slice(i * HALF, (i + 1) * HALF)
            old = jnp.where(live, sc[part, :] * factor, NEG)
            fresh = lax.dot_general(qs[part, :].astype(BF), new_k, NT, preferred_element_type=F32)
            fresh = jnp.where(mine & (fresh_col < (s + 1) * HALF), fresh * factor, NEG)
            top = jnp.max(jnp.maximum(old, fresh), axis=1, keepdims=True)
            old = jnp.exp(old - top)
            fresh = jnp.exp(fresh - top)
            total = jnp.sum(old + fresh, axis=1, keepdims=True)
            sc[part, :] = (old / total).astype(BF).astype(F32)
            mx[part, :] = jnp.dot((fresh / total).astype(BF), new_v, preferred_element_type=F32)

        def old_values(r, carry):
            p = sc[pl.ds(r, nq, stride=HALF), :].astype(BF)
            mx[pl.ds(r, nq, stride=HALF), :] += jnp.dot(
                p, cache[h * HALF + r, :, HD:], preferred_element_type=F32
            )
            return carry

        lax.fori_loop(0, HALF, old_values, 0, unroll=32)
        return jnp.concatenate(
            [mx[i * HTOK : (i + 1) * HTOK, :].astype(BF) for i in range(QPK)], axis=1
        )

    def partial_out(mixed, index):
        block = wo[pl.ds(index * 8, 8)].reshape(8 * DEEP, OUTC)
        return lax.dot_general(mixed, block, NT, preferred_element_type=F32)

    def outputs(h, mixed):
        rows, there = rows_of(h), pl.ds(h * HTOK, HTOK)
        for j, dx in enumerate((2, 1, 3, 0)):
            osb[j, rows] = partial_out(mixed, 2 * lax.rem(x + dx, NX) + 1 - c).astype(BF)
            send(osb.at[j, there], orb.at[j, there], ods.at[j, h], od.at[j, h], dev(flip=True))
        for j, dx in enumerate((2, 1, 3, 0)):
            total = partial_out(mixed, 2 * lax.rem(x + dx, NX) + c)
            wait(orb.at[j, there], od.at[j, h])
            total += orb[j, rows].astype(F32)
            if j < 3:
                xsb[j, rows] = total.astype(BF)
                send(xsb.at[j, there], xrb.at[j, there], xss.at[j, h], xr.at[j, h], dev(dx=dx))
            else:
                acc[rows, :] = total

    def finish(h):
        rows = rows_of(h)
        for j in (1, 2, 0):
            wait(xrb.at[j, pl.ds(h * HTOK, HTOK)], xr.at[j, h])
        total = acc[rows, :]
        for j in range(3):
            total += xrb[j, rows].astype(F32)
        hid[:, h * HALF : (h + 1) * HALF, :] = total.astype(BF).reshape(STEPS, HALF, FEAT)

    mixed = attention(0)
    run("first")
    wait(wo.at[0:32, pl.ds(0, ACUT)], oy)
    outputs(0, mixed)
    mixed = attention(1)
    outputs(1, mixed)
    finish(0)
    finish(1)
    back = pltpu.make_async_copy(hid, out_ref, loc_sem.at[0])
    back.start()

    wait(wq.at[0:15], zsend)
    wait(wo.at[0:63], osend)
    wait(ssb.at[0:7], ss_sem.at[0])

    @pl.when(hub)
    def _():
        wait(xs, hsend.at[0])

    @pl.when(relay)
    def _():
        wait(xs.at[0], hsend.at[0])

    @pl.when(jnp.logical_not(leaf))
    def _():
        wait(xs, hsend.at[1])

    @pl.when(jnp.logical_not(hub))
    def _():
        wait(hg, hsend.at[2])

    for h in (0, 1):
        there = pl.ds(h * HTOK, HTOK)
        for j in range(3):
            wait(ps.at[j, there], rss.at[j, h])
            wait(xsb.at[j, there], xss.at[j, h])
        for j in range(4):
            wait(osb.at[j, there], ods.at[j, h])
    back.wait()


def on_device(hidden, cache, lengths, norm_gain, w_qkv, qkv_bias, w_out):
    half = np.arange(HD // 2, dtype=np.float32) * np.float32(2.0 / HD)
    freq = np.power(np.float32(ROPE_BASE), -half).astype(np.float32)
    freq = jnp.asarray(np.concatenate([freq, freq])[None, :])
    dma = pltpu.SemaphoreType.DMA
    hbm = pl.BlockSpec(memory_space=pl.ANY)
    nq = STEPS * QPK * HALF
    return pl.pallas_call(
        kernel,
        out_shape=jax.ShapeDtypeStruct((STEPS, ROWS, FEAT), BF),
        in_specs=[hbm] * 8,
        out_specs=hbm,
        scratch_shapes=[
            pltpu.VMEM((8 * FEAT // HD, HD), F32),
            pltpu.VMEM((FEAT // HD, HD), F32),
            pltpu.VMEM((1, ROWS), jnp.int32),
            pltpu.VMEM((1, HD), F32),
            pltpu.VMEM((STEPS, ROWS, FEAT), BF),
            pltpu.VMEM((ROWS, 128, 2 * HD), BF),
            pltpu.VMEM((TOK, FEAT), BF),
            pltpu.VMEM((2, NY, TOK, FEAT), BF),
            pltpu.VMEM((NZ, DEEP, FEAT), BF),
            pltpu.VMEM((NY * NZ, DEEP, OUTC), BF),
            pltpu.VMEM((8, 8, TOK), F32),
            pltpu.VMEM((3, TOK, FEAT), BF),
            pltpu.VMEM((3, TOK, FEAT), BF),
            pltpu.VMEM((4, TOK, FEAT), BF),
            pltpu.VMEM((4, TOK, FEAT), BF),
            pltpu.VMEM((3, TOK, FEAT), BF),
            pltpu.VMEM((3, TOK, FEAT), BF),
            pltpu.VMEM((nq, HD), F32),
            pltpu.VMEM((nq, HD), F32),
            pltpu.VMEM((nq, HD), F32),
            pltpu.VMEM((TOK, HD), F32),
            pltpu.VMEM((TOK, HD), F32),
            pltpu.VMEM((TOK, HD), F32),
            pltpu.VMEM((TOK, FEAT), F32),
            dma((8,)),
            dma((NY, 2)),
            dma((2, NY, 2)),
            dma((2, NY, 2)),
            dma((2, NY, 2)),
            dma((3,)),
            dma((2, 8, len(ZCUTS))),
            dma,
            dma((2,)),
            dma((3, 2)),
            dma((3, 2)),
            dma((2, 8)),
            dma((2, 4, 8)),
            dma((4,)),
            dma((2, 9)),
            dma,
            dma,
            dma((4, 2)),
            dma((4, 2)),
            dma((3, 2)),
            dma((3, 2)),
        ],
        compiler_params=pltpu.CompilerParams(
            collective_id=0, has_side_effects=True, vmem_limit_bytes=56 * 2**20
        ),
    )(
        hidden,
        cache.reshape(ROWS, 128, 2 * HD),
        lengths.reshape(1, ROWS),
        norm_gain.reshape(8 * FEAT // HD, HD),
        w_qkv,
        qkv_bias.reshape(FEAT // HD, HD),
        w_out,
        freq,
    )


def solution(mesh):
    placed = (
        P(None, ("group", "dp"), "tensor"),
        P(("group", "dp"), "tensor", None, None),
        P(("group", "dp")),
        P(),
        P(("group", "dp"), "tensor"),
        P("tensor"),
        P(("group", "dp"), "tensor"),
    )
    return jax.shard_map(
        on_device,
        mesh=mesh,
        in_specs=placed,
        out_specs=P(None, ("group", "dp"), "tensor"),
        check_vma=False,
    )
```

```python
import functools

import jax
import jax.numpy as jnp
import numpy as np
from jax import lax
from jax.experimental import pallas as pl
from jax.experimental.pallas import tpu as pltpu
from jax.sharding import PartitionSpec as P

MESH = pl.DeviceIdType.MESH
BF, F32 = jnp.bfloat16, jnp.float32
NT = (((1,), (1,)), ((), ()))
ROPE_BASE = 1000000.0
NEG = -1e30
EPS = 1e-6
NY, NZ, NX = 4, 16, 4
ROWS = 64
STEPS = 4
TOK = STEPS * ROWS
HD = 128
HALF = 32
HTOK = STEPS * HALF
QPK = 3
DEEP = 80
FEAT = 640
OUTC = QPK * HD
ACUT = 64
ZCUTS = ((0, 32), (32, 32), (64, 16))
OFFS = (0, 1, 3, 2)
PLAN = {
    1: [("oa", 1), ("oy", 1), ("of", 0), ("hub", 1, 0), ("hub", 2, 0), ("relay", 0, 0)],
    2: [("oa", 2), ("oy", 2), ("of", 1), ("hub", 1, 1), ("hub", 2, 1), ("hub", 3, 0), ("relay", 0, 1), ("ob", 0)],
    3: [("oa", 3), ("oy", 3), ("of", 2), ("hub", 3, 1), ("relay", 1, 0), ("relay", 2, 0), ("far", 0, 0), ("far", 0, 1), ("rope", 0, 0), ("rope", 0, 1), ("ob", 1)],
    4: [("oa", 4), ("oy", 4), ("of", 3), ("relay", 1, 1), ("relay", 2, 1), ("far", 1, 0), ("far", 2, 0), ("rope", 0, 2), ("rope", 0, 3), ("ob", 2)],
    5: [("oa", 5), ("oy", 5), ("of", 4), ("relay", 3, 0), ("relay", 3, 1), ("rope", 1, 0), ("rope", 1, 1), ("ob", 3)],
    6: [("oa", 6), ("oy", 6), ("of", 5), ("far", 1, 1), ("far", 2, 1), ("far", 3, 0), ("far", 3, 1), ("rope", 1, 2), ("rope", 1, 3), ("ob", 4)],
    7: [("oa", 7), ("oy", 7), ("of", 6), ("ob", 5)],
    8: [("oa", 8), ("oy", 8), ("of", 7), ("ob", 6)],
    "sent": [("of", 8)],
    "back": [("ob", 7)],
    "first": [("ob", 8)],
}


def kernel(
    hidden_ref, cache_ref, lens_ref, gain_ref, wq_ref, bias_ref, wo_ref, freq_ref, out_ref,
    gain, bias, lens, freq, hid, cache, hg, xs, wq, wo, ssb, ps, pr, rf, osb, orb, xsb, xrb, xf, qs, sc, mx, rope_c, rope_s, rcol, acc,
    loc_sem, h1, hx, hs, hh, hsend, zs, zsend, ss_sem, rs, rss, rfs, oa, ob, oby, oyf, oy, osend, od, ods, xr, xss, xfs,
):
    g, d, t = lax.axis_index("group"), lax.axis_index("dp"), lax.axis_index("tensor")
    y, z = lax.rem(g, 4), (g // 4) * 8 + d
    x, c = t // 2, lax.rem(t, 2)

    def dev(dy=0, dz=0, dx=0, flip=False):
        yy, zz, xx = lax.rem(y + dy + NY, NY), lax.rem(z + dz + NZ, NZ), lax.rem(x + dx + NX, NX)
        return ((zz // 8) * 4 + yy, lax.rem(zz, 8), 2 * xx + ((1 - c) if flip else c))

    def slot(dy=0, dz=0):
        yy, zz = lax.rem(y + dy + NY, NY), lax.rem(z + dz + NZ, NZ)
        return ((zz // 8) * 4 + yy) * 8 + lax.rem(zz, 8)

    def send(src, dst, ssem, rsem, where):
        pltpu.make_async_remote_copy(
            src_ref=src, dst_ref=dst, send_sem=ssem, recv_sem=rsem, device_id=where, device_id_type=MESH
        ).start()

    def wait(ref, sem):
        pltpu.make_async_copy(ref, ref, sem).wait()

    loads = [
        pltpu.make_async_copy(hidden_ref, hid, loc_sem.at[0]),
        pltpu.make_async_copy(wq_ref, wq.at[z], loc_sem.at[1]),
        pltpu.make_async_copy(wo_ref, wo.at[slot()], loc_sem.at[2]),
        pltpu.make_async_copy(cache_ref, cache, loc_sem.at[3]),
        pltpu.make_async_copy(gain_ref, gain, loc_sem.at[4]),
        pltpu.make_async_copy(bias_ref, bias, loc_sem.at[5]),
        pltpu.make_async_copy(lens_ref, lens, loc_sem.at[6]),
        pltpu.make_async_copy(freq_ref, freq, loc_sem.at[7]),
    ]
    for copy in loads[1:2] + loads[:1] + loads[4:] + loads[2:4]:
        copy.start()
    barrier = pltpu.get_barrier_semaphore()
    friends = [dev(dy=1), dev(dy=2), dev(dy=3), dev(dz=1), dev(dz=-1), dev(flip=True)]
    for dx in (1, 2, 3):
        friends += [dev(dx=dx), dev(dx=dx, flip=True)]
    for friend in friends:
        pl.semaphore_signal(barrier, inc=1, device_id=friend, device_id_type=MESH)

    hub = (c == lax.rem(y, 2)) & (lax.rem(x, 2) == y // 2)
    relay = (c == lax.rem(y, 2)) & (lax.rem(x, 2) != y // 2)
    leaf = c != lax.rem(y, 2)
    kb = x // 2

    loads[1].wait()
    pl.semaphore_wait(barrier, len(friends))

    pieces = len(ZCUTS)

    def z_part(zz, piece):
        lo, n = ZCUTS[piece]
        return wq.at[zz, pl.ds(lo, n)]

    def z_send(way, zz, piece, k):
        send(z_part(zz, piece), z_part(zz, piece), zsend, zs.at[way, k - 1, piece], dev(dz=1 if way == 0 else -1))

    def z_last(way, piece):
        return (piece < pieces // 2) == (way == 1)

    def z_step(k):
        for piece in range(pieces):
            for way in (0, 1):
                if k == 8 and not z_last(way, piece):
                    continue
                zz = lax.rem(z + (NZ - k if way == 0 else k), NZ)
                wait(z_part(zz, piece), zs.at[way, k - 1, piece])
                if k < 7 or (k == 7 and z_last(way, piece)):
                    z_send(way, zz, piece, k + 1)

    def h_part(kbs, j, h, lo=0, n=HTOK):
        return xs.at[kbs, lax.rem(y + OFFS[j], NY), pl.ds(h * HTOK + lo, n)]

    def hub_event(j, h):
        @pl.when(hub)
        def _():
            part = h_part(kb, j, h)
            if j:
                wait(part, h1.at[j, h])
            send(part, part, hsend.at[0], hx.at[kb, j, h], dev(dx=1))
            send(part, part, hsend.at[0], hx.at[kb, j, h], dev(dx=-1))
            send(part, part, hsend.at[1], hs.at[kb, j, h], dev(flip=True))

    def relay_event(j, h):
        @pl.when(relay)
        def _():
            for side in (-1, 1):
                kbs = lax.rem(x + side + NX, NX) // 2
                part = h_part(kbs, j, h)
                wait(part, hx.at[kbs, j, h])
                far = 0 if side == -1 else 1
                piece = h_part(kbs, j, h, far * (HTOK // 2), HTOK // 2)
                send(piece, piece, hsend.at[0], hh.at[far, j, h], dev(dx=-side))
                send(part, part, hsend.at[1], hs.at[kbs, j, h], dev(flip=True))

    def far_event(j, h):
        @pl.when(hub)
        def _():
            for far in (0, 1):
                wait(h_part(1 - kb, j, h, far * (HTOK // 2), HTOK // 2), hh.at[far, j, h])
            part = h_part(1 - kb, j, h)
            send(part, part, hsend.at[1], hs.at[1 - kb, j, h], dev(flip=True))

    def o_y(k, way):
        part = wo.at[slot(dz=-k if way == 0 else k), pl.ds(0, ACUT)]
        send(part, part, osend, oyf.at[0, k] if way == 0 and k < 8 else oy, dev(dy=1))
        send(part, part, osend, oyf.at[1, k] if (way == 1 and k > 0) or k == 8 else oy, dev(dy=-1))

    def o_yfwd(k):
        for way in (0, 1):
            if k == 0 and way == 1 or k == 8 and way == 0:
                continue
            part = wo.at[slot(dy=-1 if way == 0 else 1, dz=-k if way == 0 else k), pl.ds(0, ACUT)]
            wait(part, oyf.at[way, k])
            send(part, part, osend, oy, dev(dy=1 if way == 0 else -1))

    def o_zsend(way, ref, sem):
        send(ref, ref, osend, sem, dev(dz=1 if way == 0 else -1))

    def o_start():
        part = wo.at[slot(), pl.ds(ACUT, DEEP - ACUT)]
        for j in (3, 1, 2):
            send(part, part, osend, oby.at[j], dev(dy=OFFS[j]))
        part = wo.at[slot(), pl.ds(0, ACUT)]
        for way in (0, 1):
            o_zsend(way, part, oa.at[way, 0])
        o_y(0, 0)

    def ob_start():
        for j in (0, 1, 2, 3):
            part = wo.at[slot(dy=-OFFS[j]), pl.ds(ACUT, DEEP - ACUT)]
            if j:
                wait(part, oby.at[j])
            for way in (0, 1):
                o_zsend(way, part, ob.at[way, j, 0])

    acuts = ((0, 32), (32, 32))

    def oa_step(k):
        for way in (0, 1):
            home = slot(dz=-k if way == 0 else k)
            lo, n = acuts[way] if k == 8 else (0, ACUT)
            wait(wo.at[home, pl.ds(lo, n)], oa.at[way, k - 1])
            if k < 8:
                lo, n = acuts[way] if k == 7 else (0, ACUT)
                o_zsend(way, wo.at[home, pl.ds(lo, n)], oa.at[way, k])

    def oa_y(k):
        for way in (0, 1):
            if k < 8 or way == 0:
                o_y(k, way)

    def ob_step(k):
        for j in range(4):
            for way in (0, 1):
                if k == 8 and j % 2 != way:
                    continue
                part = wo.at[slot(dy=-OFFS[j], dz=-k if way == 0 else k), pl.ds(ACUT, DEEP - ACUT)]
                wait(part, ob.at[way, j, k - 1])
                if k < 7 or (k == 7 and j % 2 == way):
                    o_zsend(way, part, ob.at[way, j, k])

    for piece in range(pieces):
        for way in (0, 1):
            z_send(way, z, piece, 1)
    loads[0].wait()
    loads[4].wait()
    for i in range(FEAT // HD):
        cols = slice(i * HD, (i + 1) * HD)
        row = gain[pl.ds(t * (FEAT // HD) + i, 1), :]
        for h in (0, 1):
            part = hid[:, h * HALF : (h + 1) * HALF, cols].reshape(HTOK, HD)
            hg[h * HTOK : (h + 1) * HTOK, cols] = (part.astype(F32) * row).astype(BF)

    @pl.when(hub)
    def _():
        xs[kb, y] = hg[...]

    back_y = lax.rem(y - lax.rem(t, NY) + NY, NY)
    order = lax.rem(back_y * (5 * back_y - 3) // 2, NY)

    @pl.when(jnp.logical_not(hub))
    def _():
        for h in (0, 1):
            rows = pl.ds(h * HTOK, HTOK)
            send(hg.at[rows], xs.at[kb, y, rows], hsend.at[2], h1.at[order, h], dev(dy=-back_y))

    hub_event(0, 0)
    hub_event(0, 1)
    loads[2].wait()
    o_start()
    ones = jnp.ones((8, FEAT), F32)
    for h in (0, 1):
        raw = hid[:, h * HALF : (h + 1) * HALF, :].reshape(HTOK, FEAT).astype(F32)
        ssb[t, :, h * HTOK : (h + 1) * HTOK] = lax.dot_general(
            ones, raw * raw, NT, preferred_element_type=F32, precision=lax.Precision.HIGHEST
        )
    for friend in friends[5:]:
        send(ssb.at[t], ssb.at[t], ss_sem.at[0], ss_sem.at[1], friend)

    eye = (
        lax.broadcasted_iota(jnp.int32, (ROWS, ROWS), 0) == lax.broadcasted_iota(jnp.int32, (ROWS, ROWS), 1)
    ).astype(BF)
    loads[6].wait()
    loads[7].wait()
    lens_b = lax.dot_general(
        eye,
        jnp.broadcast_to(lens[...].astype(F32), (HD, ROWS)).astype(BF),
        NT,
        preferred_element_type=F32,
    )
    lane = lax.broadcasted_iota(jnp.int32, (HALF, HD), 1)

    def rope_table(h, s):
        rows = slice((h * STEPS + s) * HALF, (h * STEPS + s + 1) * HALF)
        angle = (lens_b[h * HALF : (h + 1) * HALF, :] + float(s)) * freq[...]
        rope_c[rows, :] = jnp.cos(angle)
        sine = jnp.sin(angle)
        rope_s[rows, :] = jnp.where(lane < HD // 2, -sine, sine)

    events = {
        "hub": hub_event,
        "relay": relay_event,
        "far": far_event,
        "oa": oa_step,
        "oy": oa_y,
        "of": o_yfwd,
        "ob": lambda k: ob_step(k) if k else ob_start(),
        "rope": rope_table,
    }

    def run(key):
        for name, *what in PLAN[key]:
            events[name](*what)

    for k in range(1, 9):
        z_step(k)
        run(k)

    @pl.when(leaf)
    def _():
        for j in range(4):
            for kk in (0, 1):
                for h in (0, 1):
                    wait(h_part(kk, j, h), hs.at[kk, j, h])

    def product(ys):
        total = jnp.zeros((TOK, FEAT), F32)
        for kk in (0, 1):
            total += jnp.dot(
                xs[kk, ys], wq[kk * 8 : (kk + 1) * 8].reshape(8 * DEEP, FEAT), preferred_element_type=F32
            )
        return total

    def rows_of(h):
        return slice(h * HTOK, (h + 1) * HTOK)

    quarter = HTOK // 2

    def r_rows(h, sub):
        return pl.ds(h * HTOK + sub * quarter, quarter)

    def r_far(h):
        for way, dy in ((0, 1), (1, -1)):
            part = ps.at[2, r_rows(h, way)]
            send(part, rf.at[way, h], rss.at[2, h, way], rfs.at[way, h], dev(dy=dy))

    def r_near(h, way, sub):
        rows = r_rows(h, sub)
        send(ps.at[way, rows], pr.at[way, rows], rss.at[way, h, sub], rs.at[way, h, sub], dev(dy=1 if way == 0 else -1))

    def r_join(h):
        for way in (0, 1):
            rows = slice(h * HTOK + way * quarter, h * HTOK + (way + 1) * quarter)
            wait(rf.at[way, h], rfs.at[way, h])
            ps[way, rows] = (ps[way, rows].astype(F32) + rf[way, h].astype(F32)).astype(BF)
            r_near(h, way, way)

    ps[2] = product(lax.rem(y + 2, NY)).astype(BF)
    r_far(0)
    ps[0] = product(lax.rem(y + 1, NY)).astype(BF)
    r_near(0, 0, 1)
    ps[1] = product(lax.rem(y + 3, NY)).astype(BF)
    r_near(0, 1, 0)
    r_far(1)
    acc[...] = product(y)
    r_join(0)
    for way in (0, 1):
        r_near(1, way, 1 - way)
    run("sent")
    r_join(1)

    wait(ssb.at[0:7], ss_sem.at[1])
    whole = jnp.sum(ssb[...], axis=0)[0:1, :] * (1.0 / (8 * FEAT))
    scale = lax.rsqrt(whole + EPS)
    eye_t = (
        lax.broadcasted_iota(jnp.int32, (TOK, TOK), 0) == lax.broadcasted_iota(jnp.int32, (TOK, TOK), 1)
    ).astype(F32)
    rcol[...] = lax.dot_general(
        eye_t,
        jnp.broadcast_to(scale, (HD, TOK)),
        NT,
        preferred_element_type=F32,
        precision=lax.Precision.HIGHEST,
    )
    run("back")
    loads[5].wait()
    loads[3].wait()

    nq = STEPS * QPK
    factor = HD ** (-0.5)
    span = lax.broadcasted_iota(jnp.int32, (HALF, HD), 1).astype(F32)
    fresh_row = lax.broadcasted_iota(jnp.int32, (HALF, HTOK), 0)
    fresh_col = lax.broadcasted_iota(jnp.int32, (HALF, HTOK), 1)
    mine = lax.rem(fresh_col, HALF) == fresh_row

    def attention(h):
        rows = rows_of(h)
        for sub in (0, 1):
            for way in (0, 1):
                wait(pr.at[way, r_rows(h, sub)], rs.at[way, h, sub])

        def head(i):
            cols = slice(i * HD, (i + 1) * HD)
            total = acc[rows, cols]
            for way in (0, 1):
                total += pr[way, rows, cols].astype(F32)
            return total * rcol[rows, :] + bias[i : i + 1, :]

        def rotate(v):
            return v * rope_c[rows, :] + pltpu.roll(v, HD // 2, 1) * rope_s[rows, :]

        for i in range(QPK):
            qs[i * HTOK : (i + 1) * HTOK, :] = rotate(head(i)).astype(BF).astype(F32)
        new_k = rotate(head(QPK)).astype(BF)
        new_v = head(QPK + 1).astype(BF)

        def old_scores(r, carry):
            q = qs[pl.ds(r, nq, stride=HALF), :].astype(BF)
            sc[pl.ds(r, nq, stride=HALF), :] = lax.dot_general(
                q, cache[h * HALF + r, :, 0:HD], NT, preferred_element_type=F32
            )
            return carry

        lax.fori_loop(0, HALF, old_scores, 0, unroll=32)
        live = span < lens_b[h * HALF : (h + 1) * HALF, :]
        for i in range(nq):
            s = i % STEPS
            part = slice(i * HALF, (i + 1) * HALF)
            old = jnp.where(live, sc[part, :] * factor, NEG)
            fresh = lax.dot_general(qs[part, :].astype(BF), new_k, NT, preferred_element_type=F32)
            fresh = jnp.where(mine & (fresh_col < (s + 1) * HALF), fresh * factor, NEG)
            top = jnp.max(jnp.maximum(old, fresh), axis=1, keepdims=True)
            old = jnp.exp(old - top)
            fresh = jnp.exp(fresh - top)
            total = jnp.sum(old + fresh, axis=1, keepdims=True)
            sc[part, :] = (old / total).astype(BF).astype(F32)
            mx[part, :] = jnp.dot((fresh / total).astype(BF), new_v, preferred_element_type=F32)

        def old_values(r, carry):
            p = sc[pl.ds(r, nq, stride=HALF), :].astype(BF)
            mx[pl.ds(r, nq, stride=HALF), :] += jnp.dot(
                p, cache[h * HALF + r, :, HD:], preferred_element_type=F32
            )
            return carry

        lax.fori_loop(0, HALF, old_values, 0, unroll=32)
        return jnp.concatenate(
            [mx[i * HTOK : (i + 1) * HTOK, :].astype(BF) for i in range(QPK)], axis=1
        )

    def partial_out(mixed, index):
        block = wo[pl.ds(index * 8, 8)].reshape(8 * DEEP, OUTC)
        return lax.dot_general(mixed, block, NT, preferred_element_type=F32)

    def x_near(h, way, sub):
        rows = r_rows(h, sub)
        send(
            xsb.at[1 + way, rows], xrb.at[way, rows], xss.at[1 + way, h, sub], xr.at[way, h, sub],
            dev(dx=1 if way == 0 else -1),
        )

    def x_join(h):
        for way in (0, 1):
            rows = slice(h * HTOK + way * quarter, h * HTOK + (way + 1) * quarter)
            wait(xf.at[way, h], xfs.at[way, h])
            xsb[1 + way, rows] = (xsb[1 + way, rows].astype(F32) + xf[way, h].astype(F32)).astype(BF)
            x_near(h, way, way)

    def outputs(h, mixed):
        rows, there = rows_of(h), pl.ds(h * HTOK, HTOK)
        for j, dx in enumerate((2, 1, 3, 0)):
            osb[j, rows] = partial_out(mixed, 2 * lax.rem(x + dx, NX) + 1 - c).astype(BF)
            send(osb.at[j, there], orb.at[j, there], ods.at[j, h], od.at[j, h], dev(flip=True))
        for j, dx in enumerate((2, 1, 3, 0)):
            total = partial_out(mixed, 2 * lax.rem(x + dx, NX) + c)
            wait(orb.at[j, there], od.at[j, h])
            total += orb[j, rows].astype(F32)
            if j < 3:
                xsb[j, rows] = total.astype(BF)
            else:
                acc[rows, :] = total
            if j == 0:
                for way, step in ((0, 1), (1, -1)):
                    send(xsb.at[0, r_rows(h, way)], xf.at[way, h], xss.at[0, h, way], xfs.at[way, h], dev(dx=step))
            elif j < 3:
                x_near(h, j - 1, 2 - j)

    def finish(h):
        rows = rows_of(h)
        for sub in (0, 1):
            for way in (0, 1):
                wait(xrb.at[way, r_rows(h, sub)], xr.at[way, h, sub])
        total = acc[rows, :]
        for way in (0, 1):
            total += xrb[way, rows].astype(F32)
        hid[:, h * HALF : (h + 1) * HALF, :] = total.astype(BF).reshape(STEPS, HALF, FEAT)

    mixed = attention(0)
    run("first")
    wait(wo.at[0:32, pl.ds(0, ACUT)], oy)
    outputs(0, mixed)
    mixed = attention(1)
    x_join(0)
    outputs(1, mixed)
    x_join(1)
    finish(0)
    finish(1)
    back = pltpu.make_async_copy(hid, out_ref, loc_sem.at[0])
    back.start()

    wait(wq.at[0:15], zsend)
    wait(wo.at[0:63], osend)
    wait(ssb.at[0:7], ss_sem.at[0])

    @pl.when(hub)
    def _():
        wait(xs, hsend.at[0])

    @pl.when(relay)
    def _():
        wait(xs.at[0], hsend.at[0])

    @pl.when(jnp.logical_not(leaf))
    def _():
        wait(xs, hsend.at[1])

    @pl.when(jnp.logical_not(hub))
    def _():
        wait(hg, hsend.at[2])

    for h in (0, 1):
        there = pl.ds(h * HTOK, HTOK)
        for j in range(3):
            for sub in (0, 1):
                wait(ps.at[j, r_rows(h, sub)], rss.at[j, h, sub])
                wait(xsb.at[j, r_rows(h, sub)], xss.at[j, h, sub])
        for j in range(4):
            wait(osb.at[j, there], ods.at[j, h])
    back.wait()


def on_device(hidden, cache, lengths, norm_gain, w_qkv, qkv_bias, w_out):
    half = np.arange(HD // 2, dtype=np.float32) * np.float32(2.0 / HD)
    freq = np.power(np.float32(ROPE_BASE), -half).astype(np.float32)
    freq = jnp.asarray(np.concatenate([freq, freq])[None, :])
    dma = pltpu.SemaphoreType.DMA
    hbm = pl.BlockSpec(memory_space=pl.ANY)
    nq = STEPS * QPK * HALF
    return pl.pallas_call(
        kernel,
        out_shape=jax.ShapeDtypeStruct((STEPS, ROWS, FEAT), BF),
        in_specs=[hbm] * 8,
        out_specs=hbm,
        scratch_shapes=[
            pltpu.VMEM((8 * FEAT // HD, HD), F32),
            pltpu.VMEM((FEAT // HD, HD), F32),
            pltpu.VMEM((1, ROWS), jnp.int32),
            pltpu.VMEM((1, HD), F32),
            pltpu.VMEM((STEPS, ROWS, FEAT), BF),
            pltpu.VMEM((ROWS, 128, 2 * HD), BF),
            pltpu.VMEM((TOK, FEAT), BF),
            pltpu.VMEM((2, NY, TOK, FEAT), BF),
            pltpu.VMEM((NZ, DEEP, FEAT), BF),
            pltpu.VMEM((NY * NZ, DEEP, OUTC), BF),
            pltpu.VMEM((8, 8, TOK), F32),
            pltpu.VMEM((3, TOK, FEAT), BF),
            pltpu.VMEM((2, TOK, FEAT), BF),
            pltpu.VMEM((2, 2, HTOK // 2, FEAT), BF),
            pltpu.VMEM((4, TOK, FEAT), BF),
            pltpu.VMEM((4, TOK, FEAT), BF),
            pltpu.VMEM((3, TOK, FEAT), BF),
            pltpu.VMEM((2, TOK, FEAT), BF),
            pltpu.VMEM((2, 2, HTOK // 2, FEAT), BF),
            pltpu.VMEM((nq, HD), F32),
            pltpu.VMEM((nq, HD), F32),
            pltpu.VMEM((nq, HD), F32),
            pltpu.VMEM((TOK, HD), F32),
            pltpu.VMEM((TOK, HD), F32),
            pltpu.VMEM((TOK, HD), F32),
            pltpu.VMEM((TOK, FEAT), F32),
            dma((8,)),
            dma((NY, 2)),
            dma((2, NY, 2)),
            dma((2, NY, 2)),
            dma((2, NY, 2)),
            dma((3,)),
            dma((2, 8, len(ZCUTS))),
            dma,
            dma((2,)),
            dma((2, 2, 2)),
            dma((3, 2, 2)),
            dma((2, 2)),
            dma((2, 8)),
            dma((2, 4, 8)),
            dma((4,)),
            dma((2, 9)),
            dma,
            dma,
            dma((4, 2)),
            dma((4, 2)),
            dma((2, 2, 2)),
            dma((3, 2, 2)),
            dma((2, 2)),
        ],
        compiler_params=pltpu.CompilerParams(
            collective_id=0, has_side_effects=True, vmem_limit_bytes=56 * 2**20
        ),
    )(
        hidden,
        cache.reshape(ROWS, 128, 2 * HD),
        lengths.reshape(1, ROWS),
        norm_gain.reshape(8 * FEAT // HD, HD),
        w_qkv,
        qkv_bias.reshape(FEAT // HD, HD),
        w_out,
        freq,
    )


def solution(mesh):
    placed = (
        P(None, ("group", "dp"), "tensor"),
        P(("group", "dp"), "tensor", None, None),
        P(("group", "dp")),
        P(),
        P(("group", "dp"), "tensor"),
        P("tensor"),
        P(("group", "dp"), "tensor"),
    )
    return jax.shard_map(
        on_device,
        mesh=mesh,
        in_specs=placed,
        out_specs=P(None, ("group", "dp"), "tensor"),
        check_vma=False,
    )
```

```python
import functools

import jax
import jax.numpy as jnp
import numpy as np
from jax import lax
from jax.experimental import pallas as pl
from jax.experimental.pallas import tpu as pltpu
from jax.sharding import PartitionSpec as P

MESH = pl.DeviceIdType.MESH
BF, F32 = jnp.bfloat16, jnp.float32
NT = (((1,), (1,)), ((), ()))
ROPE_BASE = 1000000.0
NEG = -1e30
EPS = 1e-6
NY, NZ, NX = 4, 16, 4
ROWS = 64
STEPS = 4
TOK = STEPS * ROWS
HD = 128
HALF = 32
HTOK = STEPS * HALF
QPK = 3
DEEP = 80
FEAT = 640
OUTC = QPK * HD
ACUT = 64
ZCUTS = ((0, 32), (32, 32), (64, 16))
OFFS = (0, 1, 3, 2)
PLAN = {
    1: [("oa", 1), ("oy", 1), ("of", 0), ("hub", 1, 0), ("hub", 2, 0), ("relay", 0, 0)],
    2: [("oa", 2), ("oy", 2), ("of", 1), ("hub", 1, 1), ("hub", 2, 1), ("hub", 3, 0), ("relay", 0, 1), ("ob", 0)],
    3: [("oa", 3), ("oy", 3), ("of", 2), ("hub", 3, 1), ("relay", 1, 0), ("relay", 2, 0), ("far", 0, 0), ("far", 0, 1), ("rope", 0, 0), ("rope", 0, 1), ("ob", 1)],
    4: [("oa", 4), ("oy", 4), ("of", 3), ("relay", 1, 1), ("relay", 2, 1), ("far", 1, 0), ("far", 2, 0), ("rope", 0, 2), ("rope", 0, 3), ("ob", 2)],
    5: [("oa", 5), ("oy", 5), ("of", 4), ("relay", 3, 0), ("relay", 3, 1), ("rope", 1, 0), ("rope", 1, 1), ("ob", 3)],
    6: [("oa", 6), ("oy", 6), ("of", 5), ("far", 1, 1), ("far", 2, 1), ("far", 3, 0), ("far", 3, 1), ("rope", 1, 2), ("rope", 1, 3), ("ob", 4)],
    7: [("oa", 7), ("oy", 7), ("of", 6), ("ob", 5)],
    8: [("oa", 8), ("oy", 8), ("of", 7), ("ob", 6)],
    "sent": [("of", 8)],
    "back": [("ob", 7)],
    "first": [("ob", 8)],
}


def kernel(
    hidden_ref, cache_ref, lens_ref, gain_ref, wq_ref, bias_ref, wo_ref, freq_ref, out_ref,
    gain, bias, lens, freq, hid, cache, hg, xs, wq, wo, ssb, ps, pr, rf, osb, orb, xsb, xrb, xf, qs, sc, mx, rope_c, rope_s, rcol, acc,
    loc_sem, h1, hx, hs, hh, hsend, zs, zsend, ss_sem, rs, rss, rfs, oa, ob, oby, oyf, oy, osend, od, ods, xr, xss, xfs,
):
    g, d, t = lax.axis_index("group"), lax.axis_index("dp"), lax.axis_index("tensor")
    y, z = lax.rem(g, 4), (g // 4) * 8 + d
    x, c = t // 2, lax.rem(t, 2)

    def dev(dy=0, dz=0, dx=0, flip=False):
        yy, zz, xx = lax.rem(y + dy + NY, NY), lax.rem(z + dz + NZ, NZ), lax.rem(x + dx + NX, NX)
        return ((zz // 8) * 4 + yy, lax.rem(zz, 8), 2 * xx + ((1 - c) if flip else c))

    def slot(dy=0, dz=0):
        yy, zz = lax.rem(y + dy + NY, NY), lax.rem(z + dz + NZ, NZ)
        return ((zz // 8) * 4 + yy) * 8 + lax.rem(zz, 8)

    def send(src, dst, ssem, rsem, where):
        pltpu.make_async_remote_copy(
            src_ref=src, dst_ref=dst, send_sem=ssem, recv_sem=rsem, device_id=where, device_id_type=MESH
        ).start()

    def wait(ref, sem):
        pltpu.make_async_copy(ref, ref, sem).wait()

    loads = [
        pltpu.make_async_copy(hidden_ref, hid, loc_sem.at[0]),
        pltpu.make_async_copy(wq_ref, wq.at[z], loc_sem.at[1]),
        pltpu.make_async_copy(wo_ref, wo.at[slot()], loc_sem.at[2]),
        pltpu.make_async_copy(cache_ref, cache, loc_sem.at[3]),
        pltpu.make_async_copy(gain_ref, gain, loc_sem.at[4]),
        pltpu.make_async_copy(bias_ref, bias, loc_sem.at[5]),
        pltpu.make_async_copy(lens_ref, lens, loc_sem.at[6]),
        pltpu.make_async_copy(freq_ref, freq, loc_sem.at[7]),
    ]
    for copy in loads[1:2] + loads[:1] + loads[4:] + loads[2:4]:
        copy.start()
    barrier = pltpu.get_barrier_semaphore()
    friends = [dev(dy=1), dev(dy=2), dev(dy=3), dev(dz=1), dev(dz=-1), dev(flip=True)]
    for dx in (1, 2, 3):
        friends += [dev(dx=dx), dev(dx=dx, flip=True)]
    for friend in friends:
        pl.semaphore_signal(barrier, inc=1, device_id=friend, device_id_type=MESH)

    hub = (c == lax.rem(y, 2)) & (lax.rem(x, 2) == y // 2)
    relay = (c == lax.rem(y, 2)) & (lax.rem(x, 2) != y // 2)
    leaf = c != lax.rem(y, 2)
    kb = x // 2

    loads[1].wait()
    pl.semaphore_wait(barrier, len(friends))

    pieces = len(ZCUTS)

    def z_part(zz, piece):
        lo, n = ZCUTS[piece]
        return wq.at[zz, pl.ds(lo, n)]

    def z_send(way, zz, piece, k):
        send(z_part(zz, piece), z_part(zz, piece), zsend, zs.at[way, k - 1, piece], dev(dz=1 if way == 0 else -1))

    def z_last(way, piece):
        return (piece < pieces // 2) == (way == 1)

    def z_step(k):
        for piece in range(pieces):
            for way in (0, 1):
                if k == 8 and not z_last(way, piece):
                    continue
                zz = lax.rem(z + (NZ - k if way == 0 else k), NZ)
                wait(z_part(zz, piece), zs.at[way, k - 1, piece])
                if k < 7 or (k == 7 and z_last(way, piece)):
                    z_send(way, zz, piece, k + 1)

    def h_part(kbs, j, h, lo=0, n=HTOK):
        return xs.at[kbs, lax.rem(y + OFFS[j], NY), pl.ds(h * HTOK + lo, n)]

    def hub_event(j, h):
        @pl.when(hub)
        def _():
            part = h_part(kb, j, h)
            if j:
                wait(part, h1.at[j, h])
            send(part, part, hsend.at[0], hx.at[kb, j, h], dev(dx=1))
            send(part, part, hsend.at[0], hx.at[kb, j, h], dev(dx=-1))
            send(part, part, hsend.at[1], hs.at[kb, j, h], dev(flip=True))

    def relay_event(j, h):
        @pl.when(relay)
        def _():
            for side in (-1, 1):
                kbs = lax.rem(x + side + NX, NX) // 2
                part = h_part(kbs, j, h)
                wait(part, hx.at[kbs, j, h])
                far = 0 if side == -1 else 1
                piece = h_part(kbs, j, h, far * (HTOK // 2), HTOK // 2)
                send(piece, piece, hsend.at[0], hh.at[far, j, h], dev(dx=-side))
                send(part, part, hsend.at[1], hs.at[kbs, j, h], dev(flip=True))

    def far_event(j, h):
        @pl.when(hub)
        def _():
            for far in (0, 1):
                wait(h_part(1 - kb, j, h, far * (HTOK // 2), HTOK // 2), hh.at[far, j, h])
            part = h_part(1 - kb, j, h)
            send(part, part, hsend.at[1], hs.at[1 - kb, j, h], dev(flip=True))

    def o_y(k, way):
        part = wo.at[slot(dz=-k if way == 0 else k), pl.ds(0, ACUT)]
        send(part, part, osend, oyf.at[0, k] if way == 0 and k < 8 else oy, dev(dy=1))
        send(part, part, osend, oyf.at[1, k] if (way == 1 and k > 0) or k == 8 else oy, dev(dy=-1))

    def o_yfwd(k):
        for way in (0, 1):
            if k == 0 and way == 1 or k == 8 and way == 0:
                continue
            part = wo.at[slot(dy=-1 if way == 0 else 1, dz=-k if way == 0 else k), pl.ds(0, ACUT)]
            wait(part, oyf.at[way, k])
            send(part, part, osend, oy, dev(dy=1 if way == 0 else -1))

    def o_zsend(way, ref, sem):
        send(ref, ref, osend, sem, dev(dz=1 if way == 0 else -1))

    def o_start():
        part = wo.at[slot(), pl.ds(ACUT, DEEP - ACUT)]
        for j in (3, 1, 2):
            send(part, part, osend, oby.at[j], dev(dy=OFFS[j]))
        part = wo.at[slot(), pl.ds(0, ACUT)]
        for way in (0, 1):
            o_zsend(way, part, oa.at[way, 0])
        o_y(0, 0)

    def ob_start():
        for j in (0, 1, 2, 3):
            part = wo.at[slot(dy=-OFFS[j]), pl.ds(ACUT, DEEP - ACUT)]
            if j:
                wait(part, oby.at[j])
            for way in (0, 1):
                o_zsend(way, part, ob.at[way, j, 0])

    acuts = ((0, 32), (32, 32))

    def oa_step(k):
        for way in (0, 1):
            home = slot(dz=-k if way == 0 else k)
            lo, n = acuts[way] if k == 8 else (0, ACUT)
            wait(wo.at[home, pl.ds(lo, n)], oa.at[way, k - 1])
            if k < 8:
                lo, n = acuts[way] if k == 7 else (0, ACUT)
                o_zsend(way, wo.at[home, pl.ds(lo, n)], oa.at[way, k])

    def oa_y(k):
        for way in (0, 1):
            if k < 8 or way == 0:
                o_y(k, way)

    def ob_step(k):
        for j in range(4):
            for way in (0, 1):
                if k == 8 and j % 2 != way:
                    continue
                part = wo.at[slot(dy=-OFFS[j], dz=-k if way == 0 else k), pl.ds(ACUT, DEEP - ACUT)]
                wait(part, ob.at[way, j, k - 1])
                if k < 7 or (k == 7 and j % 2 == way):
                    o_zsend(way, part, ob.at[way, j, k])

    for piece in range(pieces):
        for way in (0, 1):
            z_send(way, z, piece, 1)
    loads[0].wait()
    loads[4].wait()
    for i in range(FEAT // HD):
        cols = slice(i * HD, (i + 1) * HD)
        row = gain[pl.ds(t * (FEAT // HD) + i, 1), :]
        for h in (0, 1):
            part = hid[:, h * HALF : (h + 1) * HALF, cols].reshape(HTOK, HD)
            hg[h * HTOK : (h + 1) * HTOK, cols] = (part.astype(F32) * row).astype(BF)

    @pl.when(hub)
    def _():
        xs[kb, y] = hg[...]

    back_y = lax.rem(y - lax.rem(t, NY) + NY, NY)
    order = lax.rem(back_y * (5 * back_y - 3) // 2, NY)

    @pl.when(jnp.logical_not(hub))
    def _():
        for h in (0, 1):
            rows = pl.ds(h * HTOK, HTOK)
            send(hg.at[rows], xs.at[kb, y, rows], hsend.at[2], h1.at[order, h], dev(dy=-back_y))

    hub_event(0, 0)
    hub_event(0, 1)
    loads[2].wait()
    o_start()
    ones = jnp.ones((8, FEAT), F32)
    for h in (0, 1):
        raw = hid[:, h * HALF : (h + 1) * HALF, :].reshape(HTOK, FEAT).astype(F32)
        ssb[t, :, h * HTOK : (h + 1) * HTOK] = lax.dot_general(
            ones, raw * raw, NT, preferred_element_type=F32, precision=lax.Precision.HIGHEST
        )
    for friend in friends[5:]:
        send(ssb.at[t], ssb.at[t], ss_sem.at[0], ss_sem.at[1], friend)

    eye = (
        lax.broadcasted_iota(jnp.int32, (ROWS, ROWS), 0) == lax.broadcasted_iota(jnp.int32, (ROWS, ROWS), 1)
    ).astype(BF)
    loads[6].wait()
    loads[7].wait()
    lens_b = lax.dot_general(
        eye,
        jnp.broadcast_to(lens[...].astype(F32), (HD, ROWS)).astype(BF),
        NT,
        preferred_element_type=F32,
    )
    lane = lax.broadcasted_iota(jnp.int32, (HALF, HD), 1)

    def rope_table(h, s):
        rows = slice((h * STEPS + s) * HALF, (h * STEPS + s + 1) * HALF)
        angle = (lens_b[h * HALF : (h + 1) * HALF, :] + float(s)) * freq[...]
        rope_c[rows, :] = jnp.cos(angle)
        sine = jnp.sin(angle)
        rope_s[rows, :] = jnp.where(lane < HD // 2, -sine, sine)

    events = {
        "hub": hub_event,
        "relay": relay_event,
        "far": far_event,
        "oa": oa_step,
        "oy": oa_y,
        "of": o_yfwd,
        "ob": lambda k: ob_step(k) if k else ob_start(),
        "rope": rope_table,
    }

    def run(key):
        for name, *what in PLAN[key]:
            events[name](*what)

    for k in range(1, 9):
        z_step(k)
        run(k)

    @pl.when(leaf)
    def _():
        for j in range(4):
            for kk in (0, 1):
                for h in (0, 1):
                    wait(h_part(kk, j, h), hs.at[kk, j, h])

    def product(ys):
        total = jnp.zeros((TOK, FEAT), F32)
        for kk in (0, 1):
            total += jnp.dot(
                xs[kk, ys], wq[kk * 8 : (kk + 1) * 8].reshape(8 * DEEP, FEAT), preferred_element_type=F32
            )
        return total

    def rows_of(h):
        return slice(h * HTOK, (h + 1) * HTOK)

    quarter = HTOK // 2

    def r_rows(h, sub):
        return pl.ds(h * HTOK + sub * quarter, quarter)

    def r_far(h):
        for way, dy in ((0, 1), (1, -1)):
            part = ps.at[2, r_rows(h, way)]
            send(part, rf.at[way, h], rss.at[2, h, way], rfs.at[way, h], dev(dy=dy))

    def r_near(h, way, sub):
        rows = r_rows(h, sub)
        send(ps.at[way, rows], pr.at[way, rows], rss.at[way, h, sub], rs.at[way, h, sub], dev(dy=1 if way == 0 else -1))

    def r_join(h):
        for way in (0, 1):
            rows = slice(h * HTOK + way * quarter, h * HTOK + (way + 1) * quarter)
            wait(rf.at[way, h], rfs.at[way, h])
            ps[way, rows] = (ps[way, rows].astype(F32) + rf[way, h].astype(F32)).astype(BF)
            r_near(h, way, way)

    ps[2] = product(lax.rem(y + 2, NY)).astype(BF)
    r_far(0)
    ps[0] = product(lax.rem(y + 1, NY)).astype(BF)
    r_near(0, 0, 1)
    ps[1] = product(lax.rem(y + 3, NY)).astype(BF)
    r_near(0, 1, 0)
    r_far(1)
    acc[...] = product(y)
    r_join(0)
    for way in (0, 1):
        r_near(1, way, 1 - way)
    run("sent")
    r_join(1)

    wait(ssb.at[0:7], ss_sem.at[1])
    whole = jnp.sum(ssb[...], axis=0)[0:1, :] * (1.0 / (8 * FEAT))
    scale = lax.rsqrt(whole + EPS)
    eye_t = (
        lax.broadcasted_iota(jnp.int32, (TOK, TOK), 0) == lax.broadcasted_iota(jnp.int32, (TOK, TOK), 1)
    ).astype(F32)
    rcol[...] = lax.dot_general(
        eye_t,
        jnp.broadcast_to(scale, (HD, TOK)),
        NT,
        preferred_element_type=F32,
        precision=lax.Precision.HIGHEST,
    )
    run("back")
    loads[5].wait()
    loads[3].wait()

    nq = STEPS * QPK
    factor = HD ** (-0.5)
    span = lax.broadcasted_iota(jnp.int32, (HALF, HD), 1).astype(F32)
    fresh_row = lax.broadcasted_iota(jnp.int32, (HALF, HTOK), 0)
    fresh_col = lax.broadcasted_iota(jnp.int32, (HALF, HTOK), 1)
    mine = lax.rem(fresh_col, HALF) == fresh_row

    def attention(h):
        rows = rows_of(h)
        for sub in (0, 1):
            for way in (0, 1):
                wait(pr.at[way, r_rows(h, sub)], rs.at[way, h, sub])

        def head(i):
            cols = slice(i * HD, (i + 1) * HD)
            total = acc[rows, cols]
            for way in (0, 1):
                total += pr[way, rows, cols].astype(F32)
            return total * rcol[rows, :] + bias[i : i + 1, :]

        def rotate(v):
            return v * rope_c[rows, :] + pltpu.roll(v, HD // 2, 1) * rope_s[rows, :]

        for i in range(QPK):
            qs[i * HTOK : (i + 1) * HTOK, :] = rotate(head(i)).astype(BF).astype(F32)
        new_k = rotate(head(QPK)).astype(BF)
        new_v = head(QPK + 1).astype(BF)

        def old_scores(r, carry):
            q = qs[pl.ds(r, nq, stride=HALF), :].astype(BF)
            sc[pl.ds(r, nq, stride=HALF), :] = lax.dot_general(
                q, cache[h * HALF + r, :, 0:HD], NT, preferred_element_type=F32
            )
            return carry

        lax.fori_loop(0, HALF, old_scores, 0, unroll=32)
        live = span < lens_b[h * HALF : (h + 1) * HALF, :]
        for i in range(nq):
            s = i % STEPS
            part = slice(i * HALF, (i + 1) * HALF)
            old = jnp.where(live, sc[part, :] * factor, NEG)
            fresh = lax.dot_general(qs[part, :].astype(BF), new_k, NT, preferred_element_type=F32)
            fresh = jnp.where(mine & (fresh_col < (s + 1) * HALF), fresh * factor, NEG)
            top = jnp.max(jnp.maximum(old, fresh), axis=1, keepdims=True)
            old = jnp.exp(old - top)
            fresh = jnp.exp(fresh - top)
            total = jnp.sum(old + fresh, axis=1, keepdims=True)
            sc[part, :] = (old / total).astype(BF).astype(F32)
            mx[part, :] = jnp.dot((fresh / total).astype(BF), new_v, preferred_element_type=F32)

        def old_values(r, carry):
            p = sc[pl.ds(r, nq, stride=HALF), :].astype(BF)
            mx[pl.ds(r, nq, stride=HALF), :] += jnp.dot(
                p, cache[h * HALF + r, :, HD:], preferred_element_type=F32
            )
            return carry

        lax.fori_loop(0, HALF, old_values, 0, unroll=32)
        return jnp.concatenate(
            [mx[i * HTOK : (i + 1) * HTOK, :].astype(BF) for i in range(QPK)], axis=1
        )

    def partial_out(mixed, index):
        block = wo[pl.ds(index * 8, 8)].reshape(8 * DEEP, OUTC)
        return lax.dot_general(mixed, block, NT, preferred_element_type=F32)

    def x_near(h, way, sub):
        rows = r_rows(h, sub)
        send(
            xsb.at[1 + way, rows], xrb.at[way, rows], xss.at[1 + way, h, sub], xr.at[way, h, sub],
            dev(dx=1 if way == 0 else -1),
        )

    def x_join(h):
        for way in (0, 1):
            rows = slice(h * HTOK + way * quarter, h * HTOK + (way + 1) * quarter)
            wait(xf.at[way, h], xfs.at[way, h])
            xsb[1 + way, rows] = (xsb[1 + way, rows].astype(F32) + xf[way, h].astype(F32)).astype(BF)
            x_near(h, way, way)

    def outputs(h, mixed):
        rows, there = rows_of(h), pl.ds(h * HTOK, HTOK)
        def give(j, dx):
            osb[j, rows] = partial_out(mixed, 2 * lax.rem(x + dx, NX) + 1 - c).astype(BF)
            send(osb.at[j, there], orb.at[j, there], ods.at[j, h], od.at[j, h], dev(flip=True))
        steps = (2, 1, 3, 0)
        give(0, steps[0])
        for j, dx in enumerate(steps):
            if j < 3:
                give(j + 1, steps[j + 1])
            total = partial_out(mixed, 2 * lax.rem(x + dx, NX) + c)
            wait(orb.at[j, there], od.at[j, h])
            total += orb[j, rows].astype(F32)
            if j < 3:
                xsb[j, rows] = total.astype(BF)
            else:
                acc[rows, :] = total
            if j == 0:
                for way, step in ((0, 1), (1, -1)):
                    send(xsb.at[0, r_rows(h, way)], xf.at[way, h], xss.at[0, h, way], xfs.at[way, h], dev(dx=step))
            elif j < 3:
                x_near(h, j - 1, 2 - j)

    def finish(h):
        rows = rows_of(h)
        for sub in (0, 1):
            for way in (0, 1):
                wait(xrb.at[way, r_rows(h, sub)], xr.at[way, h, sub])
        total = acc[rows, :]
        for way in (0, 1):
            total += xrb[way, rows].astype(F32)
        hid[:, h * HALF : (h + 1) * HALF, :] = total.astype(BF).reshape(STEPS, HALF, FEAT)

    mixed = attention(0)
    run("first")
    wait(wo.at[0:32, pl.ds(0, ACUT)], oy)
    outputs(0, mixed)
    mixed = attention(1)
    x_join(0)
    outputs(1, mixed)
    x_join(1)
    finish(0)
    finish(1)
    back = pltpu.make_async_copy(hid, out_ref, loc_sem.at[0])
    back.start()

    wait(wq.at[0:15], zsend)
    wait(wo.at[0:63], osend)
    wait(ssb.at[0:7], ss_sem.at[0])

    @pl.when(hub)
    def _():
        wait(xs, hsend.at[0])

    @pl.when(relay)
    def _():
        wait(xs.at[0], hsend.at[0])

    @pl.when(jnp.logical_not(leaf))
    def _():
        wait(xs, hsend.at[1])

    @pl.when(jnp.logical_not(hub))
    def _():
        wait(hg, hsend.at[2])

    for h in (0, 1):
        there = pl.ds(h * HTOK, HTOK)
        for j in range(3):
            for sub in (0, 1):
                wait(ps.at[j, r_rows(h, sub)], rss.at[j, h, sub])
                wait(xsb.at[j, r_rows(h, sub)], xss.at[j, h, sub])
        for j in range(4):
            wait(osb.at[j, there], ods.at[j, h])
    back.wait()


def on_device(hidden, cache, lengths, norm_gain, w_qkv, qkv_bias, w_out):
    half = np.arange(HD // 2, dtype=np.float32) * np.float32(2.0 / HD)
    freq = np.power(np.float32(ROPE_BASE), -half).astype(np.float32)
    freq = jnp.asarray(np.concatenate([freq, freq])[None, :])
    dma = pltpu.SemaphoreType.DMA
    hbm = pl.BlockSpec(memory_space=pl.ANY)
    nq = STEPS * QPK * HALF
    return pl.pallas_call(
        kernel,
        out_shape=jax.ShapeDtypeStruct((STEPS, ROWS, FEAT), BF),
        in_specs=[hbm] * 8,
        out_specs=hbm,
        scratch_shapes=[
            pltpu.VMEM((8 * FEAT // HD, HD), F32),
            pltpu.VMEM((FEAT // HD, HD), F32),
            pltpu.VMEM((1, ROWS), jnp.int32),
            pltpu.VMEM((1, HD), F32),
            pltpu.VMEM((STEPS, ROWS, FEAT), BF),
            pltpu.VMEM((ROWS, 128, 2 * HD), BF),
            pltpu.VMEM((TOK, FEAT), BF),
            pltpu.VMEM((2, NY, TOK, FEAT), BF),
            pltpu.VMEM((NZ, DEEP, FEAT), BF),
            pltpu.VMEM((NY * NZ, DEEP, OUTC), BF),
            pltpu.VMEM((8, 8, TOK), F32),
            pltpu.VMEM((3, TOK, FEAT), BF),
            pltpu.VMEM((2, TOK, FEAT), BF),
            pltpu.VMEM((2, 2, HTOK // 2, FEAT), BF),
            pltpu.VMEM((4, TOK, FEAT), BF),
            pltpu.VMEM((4, TOK, FEAT), BF),
            pltpu.VMEM((3, TOK, FEAT), BF),
            pltpu.VMEM((2, TOK, FEAT), BF),
            pltpu.VMEM((2, 2, HTOK // 2, FEAT), BF),
            pltpu.VMEM((nq, HD), F32),
            pltpu.VMEM((nq, HD), F32),
            pltpu.VMEM((nq, HD), F32),
            pltpu.VMEM((TOK, HD), F32),
            pltpu.VMEM((TOK, HD), F32),
            pltpu.VMEM((TOK, HD), F32),
            pltpu.VMEM((TOK, FEAT), F32),
            dma((8,)),
            dma((NY, 2)),
            dma((2, NY, 2)),
            dma((2, NY, 2)),
            dma((2, NY, 2)),
            dma((3,)),
            dma((2, 8, len(ZCUTS))),
            dma,
            dma((2,)),
            dma((2, 2, 2)),
            dma((3, 2, 2)),
            dma((2, 2)),
            dma((2, 8)),
            dma((2, 4, 8)),
            dma((4,)),
            dma((2, 9)),
            dma,
            dma,
            dma((4, 2)),
            dma((4, 2)),
            dma((2, 2, 2)),
            dma((3, 2, 2)),
            dma((2, 2)),
        ],
        compiler_params=pltpu.CompilerParams(
            collective_id=0, has_side_effects=True, vmem_limit_bytes=56 * 2**20
        ),
    )(
        hidden,
        cache.reshape(ROWS, 128, 2 * HD),
        lengths.reshape(1, ROWS),
        norm_gain.reshape(8 * FEAT // HD, HD),
        w_qkv,
        qkv_bias.reshape(FEAT // HD, HD),
        w_out,
        freq,
    )


def solution(mesh):
    placed = (
        P(None, ("group", "dp"), "tensor"),
        P(("group", "dp"), "tensor", None, None),
        P(("group", "dp")),
        P(),
        P(("group", "dp"), "tensor"),
        P("tensor"),
        P(("group", "dp"), "tensor"),
    )
    return jax.shard_map(
        on_device,
        mesh=mesh,
        in_specs=placed,
        out_specs=P(None, ("group", "dp"), "tensor"),
        check_vma=False,
    )
```
